512 devices in a mesh: seq: 16 (over y_lo, z), res: 32 (over x, y_hi, core).
Axes of the slice: x: 4, y: 8 (y_hi: 4, y_lo: 2; y = y_hi * 2 + y_lo), z: 8, core: 2. Of those that a mesh axis runs over, the one named last changes fastest.
Arguments:
- activations: bfloat16 [1024, 128, 768], P('seq', 'res'), may hold values from -10 to 10
- out_grad: bfloat16 [1024, 128, 768], P('seq', 'res'), may hold values from -96 to 96
- w_query: bfloat16 [768, 512], replicated, may hold values from -0.14433757 to 0.14433757
- w_key: bfloat16 [768, 512], replicated, may hold values from -0.14433757 to 0.14433757
- w_value: bfloat16 [768, 512], replicated, may hold values from -0.21875 to 0.21875
- w_output: bfloat16 [512, 768], replicated, may hold values from -0.25 to 0.25
Outputs:
- input_grad: bfloat16 [1024, 128, 768], P('seq', 'res')
The draws below stay inside these ranges and needn't reach their ends.
All inputs are finite; a program needn't handle non-finite values.
Results may differ from the reference program's by a relative error of at most 0.0085.
Values may be sent and summed in bfloat16 or wider, within the bound.
A program may use at most 64 MiB of HBM per device.

```python
import math
import jax
import jax.numpy as jnp
from jax import lax

D = 768
HEADS = 8
HEAD_DIM = 64
SEQS = 1024
RES = 128


def common_weight(key):
    normals = jax.random.normal(key, (D, HEADS * HEAD_DIM), jnp.float32)
    return jnp.clip(normals, -3.97, 3.97) * D ** (-0.5)


def draw_w_query(key, part):
    shared = common_weight(key)
    return shared.astype(jnp.bfloat16)


def draw_w_key(key, part):
    key = jax.random.fold_in(key, 12)
    independent = jnp.clip(jax.random.normal(key, (D, HEADS * HEAD_DIM), jnp.float32), -3.97, 3.97) * D ** (-0.5)
    result = independent
    result = jnp.clip(result, -3.97 * D ** (-0.5), 3.97 * D ** (-0.5))
    return result.astype(jnp.bfloat16)


def draw_activations(key, part):
    key = jax.random.fold_in(key, 13)
    key_base = jax.random.fold_in(key, 0)
    normals = jnp.clip(jax.random.normal(key_base, (SEQS, RES, D), jnp.float32), -5.0, 5.0)
    result = normals
    return result.astype(jnp.bfloat16)


def shard_levels(rng, extent, pieces, smallest, high):
    def one(axis_at, blocks):
        heights = jax.random.uniform(jax.random.fold_in(jax.random.fold_in(rng, 6), axis_at), (blocks,), jnp.float32, smallest / len(pieces), high / len(pieces))
        return jnp.repeat(jnp.exp(heights), extent[axis_at] // blocks).reshape((-1,) + (1,) * (len(extent) - axis_at - 1))

    loudness = one(*pieces[0])
    for cut in pieces[1:]:
        loudness = loudness * one(*cut)
    return loudness


def scatter_about(rng, dims, scale, reach, shards=(), dtype=jnp.bfloat16):
    drawn = jax.random.normal(rng, dims, jnp.float32) * scale
    if len(shards) > 0:
        drawn = shard_levels(rng, dims, shards, -0.22, 0.18) * drawn
    return jnp.clip(drawn, min=-reach, max=reach).astype(dtype)


def setup_inputs(seed: int = 0) -> dict:
    key_list = jax.random.split(jax.random.key(seed), 7)
    activations = draw_activations(jax.random.fold_in(key_list[6], 71), 0)
    out_grad = scatter_about(key_list[1], (SEQS, RES, D), 16.0, 96.0, ((0, 16), (1, 32)))
    w_query = draw_w_query(jax.random.fold_in(key_list[6], 71), 0)
    w_key = draw_w_key(jax.random.fold_in(key_list[6], 71), 0)
    w_value = scatter_about(key_list[4], (D, HEADS * HEAD_DIM), D ** -0.5, 0.21875)
    w_output = scatter_about(key_list[5], (HEADS * HEAD_DIM, D), (HEADS * HEAD_DIM) ** -0.5, 0.25)
    return {"activations": activations, "out_grad": out_grad, "w_query": w_query, "w_key": w_key, "w_value": w_value, "w_output": w_output}


def project(rows, weight):
    return jnp.dot(rows, weight, preferred_element_type=jnp.float32).astype(jnp.bfloat16).reshape(SEQS, RES, HEADS, HEAD_DIM)

def reference(activations, out_grad, w_query, w_key, w_value, w_output):
    flat = activations.reshape(SEQS * RES, D)
    queries = project(flat, w_query)
    key_rows = project(flat, w_key)
    values = project(flat, w_value)
    head_grad = project(out_grad.reshape(SEQS * RES, D), w_output.T)
    score_scale = 1.0 / math.sqrt(HEAD_DIM * SEQS)
    scores = score_scale * jnp.einsum('sihe,sjhe->hij', queries.astype(jnp.float32), key_rows.astype(jnp.float32))
    probability = jax.nn.softmax(scores, axis=-1)
    prob_low = probability.astype(jnp.bfloat16)
    prob_grad = jnp.einsum('sihe,sjhe->hij', head_grad.astype(jnp.float32), values.astype(jnp.float32))
    row_total = lax.optimization_barrier(jnp.sum(probability * prob_grad, axis=-1, keepdims=True))
    score_grad = (score_scale * probability * (prob_grad - row_total)).astype(jnp.bfloat16)
    query_grad = jnp.einsum('hij,sjhe->sihe', score_grad.astype(jnp.float32), key_rows.astype(jnp.float32)).astype(jnp.bfloat16)
    key_grad = jnp.einsum('hij,sihe->sjhe', score_grad.astype(jnp.float32), queries.astype(jnp.float32)).astype(jnp.bfloat16)
    value_grad = jnp.einsum('hij,sihe->sjhe', prob_low.astype(jnp.float32), head_grad.astype(jnp.float32)).astype(jnp.bfloat16)
    feature = HEADS * HEAD_DIM
    total = jnp.dot(query_grad.reshape(SEQS * RES, feature), w_query.T, preferred_element_type=jnp.float32)
    total = total + jnp.dot(key_grad.reshape(SEQS * RES, feature), w_key.T, preferred_element_type=jnp.float32)
    total = total + jnp.dot(value_grad.reshape(SEQS * RES, feature), w_value.T, preferred_element_type=jnp.float32)
    return total.astype(jnp.bfloat16).reshape(SEQS, RES, D)
```

```python
import math

import jax
import jax.numpy as jnp
from jax import lax
from jax.sharding import Mesh, PartitionSpec as P

HEADS = 8
HEAD_DIM = 64
GROUP = ("x", "yh", "core")


def project(block, weight):
    rows = block.shape[0] * block.shape[1]
    flat = block.reshape(rows, block.shape[-1])
    return jnp.dot(flat, weight, preferred_element_type=jnp.float32).astype(jnp.bfloat16)


def body(activations, out_grad, w_query, w_key, w_value, w_output):
    seqs, res, _ = activations.shape
    chunk = seqs // 4
    scale = 1.0 / math.sqrt(HEAD_DIM * seqs * lax.axis_size("seq"))

    def spread(block):
        block = block.reshape(4, chunk, res, 4, 2, HEAD_DIM)
        return block.transpose(3, 0, 4, 1, 2, 5).reshape(32, chunk * res, HEAD_DIM)

    queries = spread(project(activations, w_query))
    key_rows = spread(project(activations, w_key))
    values = spread(project(activations, w_value))
    head_grad = spread(project(out_grad, w_output.T))
    packed = jnp.concatenate([queries, key_rows, head_grad, values], axis=-1)
    packed = lax.all_to_all(packed, GROUP, split_axis=0, concat_axis=0, tiled=True)
    packed = packed.reshape(32, chunk, res, 4, HEAD_DIM)
    packed = packed.transpose(3, 1, 0, 2, 4).reshape(4, chunk, 32 * res, HEAD_DIM)
    q, k, g, v = packed[0], packed[1], packed[2], packed[3]
    parts = jnp.stack(
        [
            jnp.einsum("sie,sje->ij", q, k, preferred_element_type=jnp.float32),
            jnp.einsum("sie,sje->ij", g, v, preferred_element_type=jnp.float32),
        ]
    )
    parts = lax.psum(parts, ("seq", "yh"))
    probability = jax.nn.softmax(scale * parts[0], axis=-1)
    prob_grad = parts[1]
    row_total = jnp.sum(probability * prob_grad, axis=-1, keepdims=True)
    score_grad = (scale * probability * (prob_grad - row_total)).astype(jnp.bfloat16)
    prob_low = probability.astype(jnp.bfloat16)
    f32 = jnp.float32
    grads = jnp.stack(
        [
            jnp.einsum("ij,sje->sie", score_grad, k, preferred_element_type=f32),
            jnp.einsum("ij,sie->sje", score_grad, q, preferred_element_type=f32),
            jnp.einsum("ij,sie->sje", prob_low, g, preferred_element_type=f32),
        ]
    ).astype(jnp.bfloat16)
    grads = grads.reshape(3, chunk, 32, res, HEAD_DIM).transpose(2, 1, 3, 0, 4)
    grads = lax.all_to_all(
        grads.reshape(32, chunk * res, 3 * HEAD_DIM), GROUP, split_axis=0, concat_axis=0, tiled=True
    )
    grads = grads.reshape(4, 4, 2, chunk * res, 3, HEAD_DIM).transpose(4, 1, 3, 0, 2, 5)
    grads = grads.reshape(3, seqs * res, HEADS * HEAD_DIM)
    total = jnp.dot(grads[0], w_query.T, preferred_element_type=f32)
    total = total + jnp.dot(grads[1], w_key.T, preferred_element_type=f32)
    total = total + jnp.dot(grads[2], w_value.T, preferred_element_type=f32)
    return total.astype(jnp.bfloat16).reshape(activations.shape)


def solution(mesh):
    fine = Mesh(mesh.devices.reshape(16, 4, 4, 2), ("seq",) + GROUP)
    rows = P("seq", GROUP, None)
    return jax.shard_map(
        body,
        mesh=fine,
        in_specs=(rows, rows, P(), P(), P(), P()),
        out_specs=rows,
        check_vma=False,
    )
```

```python
import math

import jax
import jax.numpy as jnp
from jax import lax
from jax.experimental import pallas as pl
from jax.experimental.pallas import tpu as pltpu
from jax.sharding import PartitionSpec as P

MESH = pl.DeviceIdType.MESH
F32, BF16 = jnp.float32, jnp.bfloat16
D = 768
FEATURES = 512
HEAD_DIM = 64
SEQ_RUN = 16
RES = 4
ROWS = SEQ_RUN * RES
NT = (((1,), (1,)), ((), ()))
TN = (((0,), (0,)), ((), ()))


def rows_dot(a, b, dims=(((1,), (0,)), ((), ()))):
    return lax.dot_general(a, b, dims, preferred_element_type=F32)


def kernel(
    scale,
    act, og, wq_hbm, wk_hbm, wv_hbm, wo_hbm,
    out,
    wq, wk, wv, wo, og_v, xr, g_send, gr, v_roll,
    qk_send, gv_send, qk_recv, gv_recv,
    wide, z_qk, z_gv, rolled, masked,
    part, part_recv, total, total_recv, probs,
    wide_v, back_send, back_recv, out_send,
    load_sem, x_send_sem, x_recv_sem, g_send_sem, g_recv_sem,
    qk_send_sem, qk_recv_sem, gv_send_sem, gv_recv_sem, own_sem,
    part_send_sem, part_recv_sem, total_send_sem, total_recv_sem,
    probs_send_sem, probs_recv_sem, back_send_sem, back_recv_sem, back_own_sem,
    out_send_sem, out_recv_sem, out_own_sem,
):
    seq, res = lax.axis_index("seq"), lax.axis_index("res")
    ylo, z = seq // 8, seq % 8
    x, yh, core = res // 8, (res // 2) % 4, res % 2
    g = x * 2 + core
    w = yh * 2 + ylo

    def y_peer(h):
        return (seq, x * 8 + h * 2 + core)

    def head_peer(h):
        return (seq, (h // 2) * 8 + yh * 2 + h % 2)

    def z_peer(k):
        return (ylo * 8 + k, res)

    def line_peer(k):
        return ((k % 2) * 8 + z, x * 8 + (k // 2) * 2 + core)

    def run(h):
        return pl.ds(pl.multiple_of(h * SEQ_RUN, SEQ_RUN), SEQ_RUN)

    loads = [
        pltpu.make_async_copy(og, og_v, load_sem.at[0]),
        pltpu.make_async_copy(wo_hbm, wo, load_sem.at[1]),
        pltpu.make_async_copy(act.at[run(yh)], xr.at[yh], load_sem.at[2]),
        pltpu.make_async_copy(wq_hbm, wq, load_sem.at[3]),
        pltpu.make_async_copy(wk_hbm, wk, load_sem.at[4]),
        pltpu.make_async_copy(wv_hbm, wv, load_sem.at[5]),
    ]
    for load in loads:
        load.start()

    barrier = pltpu.get_barrier_semaphore()

    def greet(k, _):
        pl.semaphore_signal(barrier, inc=1, device_id=head_peer((g + k) % 8), device_id_type=MESH)
        pl.semaphore_signal(barrier, inc=1, device_id=z_peer((z + k) % 8), device_id_type=MESH)
        pl.semaphore_signal(barrier, inc=1, device_id=line_peer((w + k) % 8), device_id_type=MESH)
        return 0

    lax.fori_loop(1, 8, greet, 0)
    pl.semaphore_wait(barrier, 21)

    def x_copy(to, slot):
        return pltpu.make_async_remote_copy(
            act.at[run(to)], xr.at[slot], x_send_sem, x_recv_sem.at[slot],
            device_id=y_peer(to), device_id_type=MESH,
        )

    def g_copy(to, slot):
        return pltpu.make_async_remote_copy(
            g_send.at[to], gr.at[slot], g_send_sem, g_recv_sem.at[slot],
            device_id=y_peer(to), device_id_type=MESH,
        )

    def near_first(k):
        return k + k // 2 - 2 * (k // 3)

    def send_x(k, _):
        x_copy((yh + near_first(k)) % 4, yh).start()
        return 0

    lax.fori_loop(1, 4, send_x, 0)

    loads[0].wait()
    loads[1].wait()
    grad_rows = rows_dot(og_v[...].reshape(4 * ROWS, D), wo[...], NT).astype(BF16)
    g_send[...] = grad_rows.reshape(4, ROWS, FEATURES)

    def send_g(k, _):
        g_copy((yh + near_first(k)) % 4, yh).start()
        return 0

    lax.fori_loop(1, 4, send_g, 0)
    gr[yh] = g_send[yh]

    low_half = lax.broadcasted_iota(jnp.int32, (ROWS, 128), 1) < HEAD_DIM

    def pack(first, second, send, src):
        for p in range(4):
            a, b = first[:, p * 128 : p * 128 + 128], second[:, p * 128 : p * 128 + 128]
            send[2 * p, src] = jnp.where(low_half, a, b)
            send[2 * p + 1, src] = jnp.where(low_half, b, a)

    def spread(send, recv, send_sem, recv_sem, src, own_at):
        def one(k, _):
            to = (g + k) % 8
            pltpu.make_async_remote_copy(
                send.at[to, src], recv.at[g, src], send_sem, recv_sem,
                device_id=head_peer(to), device_id_type=MESH,
            ).start()
            return 0

        lax.fori_loop(1, 8, one, 0)
        pltpu.make_async_copy(send.at[g, src], recv.at[g, src], own_sem.at[own_at, src]).start()

    def roll_pairs(a):
        return jnp.concatenate(
            [pltpu.roll(a[:, p * 128 : p * 128 + 128], HEAD_DIM, 1) for p in range(4)], axis=1
        )

    def do_qk(src):
        rows = xr[src].reshape(ROWS, D)
        q = rows_dot(rows, wq[...]).astype(BF16)
        k = rows_dot(rows, wk[...]).astype(BF16)
        pack(q, roll_pairs(k), qk_send, src)
        spread(qk_send, qk_recv, qk_send_sem, qk_recv_sem, src, 0)
        v_roll[src] = roll_pairs(rows_dot(rows, wv[...]).astype(BF16))

    def do_gv(src):
        pack(gr[src], v_roll[src], gv_send, src)
        spread(gv_send, gv_recv, gv_send_sem, gv_recv_sem, src, 1)

    for load in loads[2:]:
        load.wait()
    do_qk(yh)
    do_gv(yh)

    def next_qk(k, _):
        src = (yh + near_first(k)) % 4
        x_copy(src, src).wait_recv()
        do_qk(src)
        return 0

    lax.fori_loop(1, 4, next_qk, 0)

    def next_gv(k, _):
        src = (yh + near_first(k)) % 4
        g_copy(src, src).wait_recv()
        do_gv(src)
        return 0

    lax.fori_loop(1, 4, next_gv, 0)

    lane = lax.broadcasted_iota(jnp.int32, (128, 128), 1)
    first = (lane // HEAD_DIM) == core
    first_scale = jnp.where(first, 1.0, 0.0).astype(BF16)

    def wait_all(send, recv, recv_sem, own_at):
        part_of = recv.at[pl.ds(0, 7)]
        pltpu.make_async_copy(part_of, part_of, recv_sem).wait()
        for src in range(4):
            pltpu.make_async_copy(send.at[g, src], recv.at[g, src], own_sem.at[own_at, src]).wait()

    def product(recv, keep):
        wide[...] = recv[...].reshape(32 * ROWS, 128).astype(F32)
        for s in range(SEQ_RUN):
            block = jnp.concatenate(
                [wide[pl.ds(s * RES + r, 32, stride=ROWS), :] for r in range(RES)], axis=0
            ).astype(BF16)
            lanes = slice(s * 128, s * 128 + 128)
            keep[:, lanes] = block
            masked[:, lanes] = block * first_scale
            rolled[:, lanes] = pltpu.roll(block, HEAD_DIM, 1)
        return rows_dot(masked[...], rolled[...], NT)

    wait_all(qk_send, qk_recv, qk_recv_sem, 0)
    part[:, 0] = product(qk_recv, z_qk).reshape(8, 16, 128)
    wait_all(gv_send, gv_recv, gv_recv_sem, 1)
    part[:, 1] = product(gv_recv, z_gv).reshape(8, 16, 128)

    def send_part(k, _):
        to = (z + k) % 8
        pltpu.make_async_remote_copy(
            part.at[to], part_recv.at[z], part_send_sem, part_recv_sem,
            device_id=z_peer(to), device_id_type=MESH,
        ).start()
        return 0

    lax.fori_loop(1, 8, send_part, 0)
    part_recv[z] = part[z]
    seven = part_recv.at[pl.ds(0, 7)]
    pltpu.make_async_copy(seven, seven, part_recv_sem).wait()
    total[...] = jnp.sum(part_recv[...], axis=0)

    def send_total(k, _):
        to = (w + k) % 8
        pltpu.make_async_remote_copy(
            total, total_recv.at[w], total_send_sem, total_recv_sem,
            device_id=line_peer(to), device_id_type=MESH,
        ).start()
        return 0

    lax.fori_loop(1, 8, send_total, 0)
    total_recv[w] = total[...]
    seven_t = total_recv.at[pl.ds(0, 7)]
    pltpu.make_async_copy(seven_t, seven_t, total_recv_sem).wait()
    sums = jnp.sum(total_recv[...], axis=0)
    scores, prob_grad = scale * sums[0], sums[1]
    grown = jnp.exp(scores - jnp.max(scores, axis=-1, keepdims=True))
    probability = grown / jnp.sum(grown, axis=-1, keepdims=True)
    row_total = jnp.sum(probability * prob_grad, axis=-1, keepdims=True)
    probs[z, 0] = (scale * probability * (prob_grad - row_total)).astype(BF16)
    probs[z, 1] = probability.astype(BF16)

    def send_probs(k, _):
        to = (z + k) % 8
        pltpu.make_async_remote_copy(
            probs.at[z], probs.at[z], probs_send_sem, probs_recv_sem,
            device_id=z_peer(to), device_id_type=MESH,
        ).start()
        return 0

    lax.fori_loop(1, 8, send_probs, 0)
    seven_p = probs.at[pl.ds(0, 7)]
    pltpu.make_async_copy(seven_p, seven_p, probs_recv_sem).wait()
    score_grad = probs[:, 0].reshape(128, 128)
    prob_low = probs[:, 1].reshape(128, 128)

    to_query = rows_dot(score_grad, z_qk[...])
    to_key = rows_dot(score_grad, z_qk[...], TN)
    to_value = rows_dot(prob_low, z_gv[...], TN)
    for s in range(SEQ_RUN):
        lanes = slice(s * 128, s * 128 + 128)
        block = jnp.where(first, to_key[:, lanes], to_query[:, lanes])
        for r in range(RES):
            wide[pl.ds(s * RES + r, 32, stride=ROWS), :] = block[r * 32 : r * 32 + 32]
    half = SEQ_RUN // 2
    for s in range(half):
        near, far = to_value[:, s * 128 : s * 128 + 128], to_value[:, (s + half) * 128 : (s + half + 1) * 128]
        block = jnp.where(first, near, pltpu.roll(far, HEAD_DIM, 1))
        for r in range(RES):
            wide_v[pl.ds(s * RES + r, 32, stride=ROWS // 2), :] = block[r * 32 : r * 32 + 32]
    back_send[:, :, :ROWS] = wide[...].astype(BF16).reshape(8, 4, ROWS, 128)
    back_send[:, :, ROWS:] = wide_v[...].astype(BF16).reshape(8, 4, ROWS // 2, 128)

    def far_first(k):
        return near_first(3 - k)

    def send_back(k, _):
        src = (yh + far_first(k)) % 4

        def one(j, _):
            to = (g + j) % 8
            pltpu.make_async_remote_copy(
                back_send.at[to, src], back_recv.at[g, src], back_send_sem, back_recv_sem.at[src],
                device_id=head_peer(to), device_id_type=MESH,
            ).start()
            return 0

        lax.fori_loop(1, 8, one, 0)
        pltpu.make_async_copy(back_send.at[g, src], back_recv.at[g, src], back_own_sem.at[src]).start()
        return 0

    lax.fori_loop(0, 4, send_back, 0)

    low_back = lax.broadcasted_iota(jnp.int32, (ROWS + ROWS // 2, 128), 1) < HEAD_DIM

    def out_copy(to, slot):
        return pltpu.make_async_remote_copy(
            out_send.at[to], out.at[run(slot)], out_send_sem, out_recv_sem.at[slot],
            device_id=y_peer(to), device_id_type=MESH,
        )

    def finish(src):
        arrived = back_recv.at[pl.ds(0, 7), src]
        pltpu.make_async_copy(arrived, arrived, back_recv_sem.at[src]).wait()
        pltpu.make_async_copy(back_send.at[g, src], back_recv.at[g, src], back_own_sem.at[src]).wait()
        dq, dk, dv = [], [], []
        for p in range(4):
            a, b = back_recv[2 * p, src], back_recv[2 * p + 1, src]
            straight = jnp.where(low_back, a, b)
            swapped = pltpu.roll(jnp.where(low_back, b, a), HEAD_DIM, 1)
            dk.append(straight[:ROWS])
            dq.append(swapped[:ROWS])
            dv.append(jnp.concatenate([straight[ROWS:], swapped[ROWS:]], axis=0))
        grad = rows_dot(jnp.concatenate(dq, axis=1), wq[...], NT)
        grad = grad + rows_dot(jnp.concatenate(dk, axis=1), wk[...], NT)
        grad = grad + rows_dot(jnp.concatenate(dv, axis=1), wv[...], NT)
        out_send[src] = grad.astype(BF16).reshape(SEQ_RUN, RES, D)

    def finish_far(k, _):
        src = (yh + far_first(k)) % 4
        finish(src)
        out_copy(src, yh).start()
        return 0

    lax.fori_loop(0, 3, finish_far, 0)
    finish(yh)
    own_out = pltpu.make_async_copy(out_send.at[yh], out.at[run(yh)], out_own_sem)
    own_out.start()

    def wait_bytes(ref, sem):
        pltpu.make_async_copy(ref, ref, sem).wait()

    wait_bytes(xr.at[pl.ds(0, 3)], x_send_sem)
    wait_bytes(gr.at[pl.ds(0, 3)], g_send_sem)
    wait_bytes(qk_send.at[pl.ds(0, 7)], qk_send_sem)
    wait_bytes(gv_send.at[pl.ds(0, 7)], gv_send_sem)
    wait_bytes(part_recv.at[pl.ds(0, 7)], part_send_sem)
    wait_bytes(total_recv.at[pl.ds(0, 7)], total_send_sem)
    wait_bytes(probs.at[pl.ds(0, 7)], probs_send_sem)
    wait_bytes(back_send.at[pl.ds(0, 7)], back_send_sem)
    wait_bytes(out_send.at[pl.ds(0, 3)], out_send_sem)

    def wait_out(k, _):
        src = (yh + k) % 4
        out_copy(src, src).wait_recv()
        return 0

    lax.fori_loop(1, 4, wait_out, 0)
    own_out.wait()


def body(activations, out_grad, w_query, w_key, w_value, w_output):
    seqs_total = activations.shape[0] * lax.axis_size("seq")
    scale = 1.0 / math.sqrt(HEAD_DIM * seqs_total)
    any_space = pl.BlockSpec(memory_space=pl.ANY)
    dma = pltpu.SemaphoreType.DMA
    vmem = pltpu.VMEM
    return pl.pallas_call(
        lambda *refs: kernel(scale, *refs),
        out_shape=jax.ShapeDtypeStruct(activations.shape, BF16),
        in_specs=[any_space] * 6,
        out_specs=any_space,
        scratch_shapes=[
            vmem((D, FEATURES), BF16),
            vmem((D, FEATURES), BF16),
            vmem((D, FEATURES), BF16),
            vmem((FEATURES, D), BF16),
            vmem((4 * SEQ_RUN, RES, D), BF16),
            vmem((4, SEQ_RUN, RES, D), BF16),
            vmem((4, ROWS, FEATURES), BF16),
            vmem((4, ROWS, FEATURES), BF16),
            vmem((4, ROWS, FEATURES), BF16),
            vmem((8, 4, ROWS, 128), BF16),
            vmem((8, 4, ROWS, 128), BF16),
            vmem((8, 4, ROWS, 128), BF16),
            vmem((8, 4, ROWS, 128), BF16),
            vmem((32 * ROWS, 128), F32),
            vmem((128, SEQ_RUN * 128), BF16),
            vmem((128, SEQ_RUN * 128), BF16),
            vmem((128, SEQ_RUN * 128), BF16),
            vmem((128, SEQ_RUN * 128), BF16),
            vmem((8, 2, 16, 128), F32),
            vmem((8, 2, 16, 128), F32),
            vmem((2, 16, 128), F32),
            vmem((8, 2, 16, 128), F32),
            vmem((8, 2, 16, 128), BF16),
            vmem((16 * ROWS, 128), F32),
            vmem((8, 4, ROWS + ROWS // 2, 128), BF16),
            vmem((8, 4, ROWS + ROWS // 2, 128), BF16),
            vmem((4, SEQ_RUN, RES, D), BF16),
            dma((6,)), dma, dma((4,)), dma, dma((4,)),
            dma, dma, dma, dma, dma((2, 4)),
            dma, dma, dma, dma,
            dma, dma, dma, dma((4,)), dma((4,)),
            dma, dma((4,)), dma,
        ],
        compiler_params=pltpu.CompilerParams(
            collective_id=0, has_side_effects=True, vmem_limit_bytes=40 * 2**20
        ),
        cost_estimate=pl.CostEstimate(
            flops=2 * 10**9, bytes_accessed=5 * 10**6, transcendentals=2048
        ),
    )(activations, out_grad, w_query, w_key, w_value, w_output)


def solution(mesh):
    rows = P("seq", "res", None)
    return jax.shard_map(
        body,
        mesh=mesh,
        in_specs=(rows, rows, P(), P(), P(), P()),
        out_specs=rows,
        check_vma=False,
    )
```

```python
import math

import jax
import jax.numpy as jnp
from jax import lax
from jax.experimental import pallas as pl
from jax.experimental.pallas import tpu as pltpu
from jax.sharding import PartitionSpec as P

MESH = pl.DeviceIdType.MESH
F32, BF16 = jnp.float32, jnp.bfloat16
D = 768
FEATURES = 512
HEAD_DIM = 64
SEQ_RUN = 16
RES = 4
ROWS = SEQ_RUN * RES
HALF = ROWS // 2
NT = (((1,), (1,)), ((), ()))
TN = (((0,), (0,)), ((), ()))


def rows_dot(a, b, dims=(((1,), (0,)), ((), ()))):
    return lax.dot_general(a, b, dims, preferred_element_type=F32)


def kernel(
    scale,
    act, og, wq_hbm, wk_hbm, wv_hbm, wo_hbm,
    out,
    wq, wk, wv, wo, og_v, xr, g_near, g_own, g_recv, qkv_send, qkv_recv,
    wide, wide_g, q_all, k_all, v_all, g_all,
    part, part_recv, total, total_recv, probs, back_send, back_recv, out_send,
    load_sem, x_send_sem, x_recv_sem, near_send_sem, near_recv_sem, near_own_sem,
    g_send_sem, g_recv_sem, g_own_sem, qkv_send_sem, qkv_recv_sem, qkv_own_sem,
    part_send_sem, part_recv_sem, total_send_sem, total_recv_sem,
    probs_send_sem, probs_recv_sem, back_send_sem, back_recv_sem, back_own_sem,
    out_send_sem, out_recv_sem, out_own_sem,
):
    seq, res = lax.axis_index("seq"), lax.axis_index("res")
    ylo, z = seq // 8, seq % 8
    x, yh, core = res // 8, (res // 2) % 4, res % 2
    g = x * 2 + core
    w = yh * 2 + ylo

    def y_peer(h):
        return (seq, x * 8 + h * 2 + core)

    def head_peer(h):
        return (seq, (h // 2) * 8 + yh * 2 + h % 2)

    def z_peer(k):
        return (ylo * 8 + k, res)

    def line_peer(k):
        return ((k % 2) * 8 + z, x * 8 + (k // 2) * 2 + core)

    def run(h):
        return pl.ds(pl.multiple_of(h * SEQ_RUN, SEQ_RUN), SEQ_RUN)

    def wait_bytes(ref, sem):
        pltpu.make_async_copy(ref, ref, sem).wait()

    loads = [
        pltpu.make_async_copy(og, og_v, load_sem.at[0]),
        pltpu.make_async_copy(wo_hbm, wo, load_sem.at[1]),
        pltpu.make_async_copy(act.at[run(yh)], xr.at[yh], load_sem.at[2]),
        pltpu.make_async_copy(wq_hbm, wq, load_sem.at[3]),
        pltpu.make_async_copy(wk_hbm, wk, load_sem.at[4]),
        pltpu.make_async_copy(wv_hbm, wv, load_sem.at[5]),
    ]
    for load in loads:
        load.start()

    barrier = pltpu.get_barrier_semaphore()

    def greet(k, _):
        pl.semaphore_signal(barrier, inc=1, device_id=head_peer((g + k) % 8), device_id_type=MESH)
        pl.semaphore_signal(barrier, inc=1, device_id=z_peer((z + k) % 8), device_id_type=MESH)
        pl.semaphore_signal(barrier, inc=1, device_id=line_peer((w + k) % 8), device_id_type=MESH)
        return 0

    lax.fori_loop(1, 8, greet, 0)

    low = lax.broadcasted_iota(jnp.int32, (HALF, 128), 1) < HEAD_DIM

    def fold(top, bottom):
        turned = pltpu.roll(bottom, HEAD_DIM, 1)
        return jnp.where(low, top, turned), jnp.where(low, turned, top)

    loads[0].wait()
    loads[1].wait()
    grad_rows = rows_dot(og_v[...].reshape(4 * ROWS, D), wo[...], NT).astype(BF16)
    for c in range(4):
        for p in range(4):
            pair = grad_rows[c * ROWS : (c + 1) * ROWS, p * 128 : p * 128 + 128]
            g_near[2 * p, c], g_near[2 * p + 1, c] = fold(pair[:HALF], pair[HALF:])

    pl.semaphore_wait(barrier, 21)

    def x_copy(to, slot):
        return pltpu.make_async_remote_copy(
            act.at[run(to)], xr.at[slot], x_send_sem.at[to], x_recv_sem.at[slot],
            device_id=y_peer(to), device_id_type=MESH,
        )

    after, before, far = (yh + 1) % 4, (yh + 3) % 4, (yh + 2) % 4
    x_copy(after, yh).start()
    x_copy(before, yh).start()

    def send_near(k, _):
        to = (g + k) % 8
        pltpu.make_async_remote_copy(
            g_near.at[to], g_own.at[g], near_send_sem, near_recv_sem,
            device_id=head_peer(to), device_id_type=MESH,
        ).start()
        return 0

    lax.fori_loop(1, 8, send_near, 0)
    near_copy = pltpu.make_async_copy(g_near.at[g], g_own.at[g], near_own_sem)
    near_copy.start()

    def do_qkv(src):
        rows = xr[src].reshape(ROWS, D)
        for j, weight in enumerate((wq, wk, wv)):
            a = rows_dot(rows, weight[...]).astype(BF16)
            for p in range(4):
                pair = a[:, p * 128 : p * 128 + 128]
                even, odd = fold(pair[:HALF], pair[HALF:])
                qkv_send[2 * p, src, j * HALF : (j + 1) * HALF] = even
                qkv_send[2 * p + 1, src, j * HALF : (j + 1) * HALF] = odd

        def one(k, _):
            to = (g + k) % 8
            pltpu.make_async_remote_copy(
                qkv_send.at[to, src], qkv_recv.at[g, src], qkv_send_sem, qkv_recv_sem,
                device_id=head_peer(to), device_id_type=MESH,
            ).start()
            return 0

        lax.fori_loop(1, 8, one, 0)
        pltpu.make_async_copy(qkv_send.at[g, src], qkv_recv.at[g, src], qkv_own_sem.at[src]).start()

    for load in loads[2:]:
        load.wait()
    do_qkv(yh)

    x_copy(after, yh).wait_send()
    x_copy(before, yh).wait_send()
    x_copy(far, yh).start()

    def near_qkv(k, _):
        src = (yh + 1 + 2 * k) % 4
        x_copy(src, src).wait_recv()
        do_qkv(src)
        return 0

    lax.fori_loop(0, 2, near_qkv, 0)

    def g_copy(to, slot):
        return pltpu.make_async_remote_copy(
            g_own.at[:, to], g_recv.at[:, slot], g_send_sem, g_recv_sem,
            device_id=y_peer(to), device_id_type=MESH,
        )

    wait_bytes(g_own.at[pl.ds(0, 7)], near_recv_sem)
    near_copy.wait()
    x_copy(far, yh).wait_send()
    g_copy(after, yh).start()
    g_copy(before, yh).start()
    g_copy(far, yh).start()
    own_g = pltpu.make_async_copy(g_own.at[:, yh], g_recv.at[:, yh], g_own_sem)
    own_g.start()

    x_copy(far, far).wait_recv()
    do_qkv(far)

    wait_bytes(qkv_recv.at[pl.ds(0, 7)], qkv_recv_sem)
    for src in range(4):
        pltpu.make_async_copy(qkv_send.at[g, src], qkv_recv.at[g, src], qkv_own_sem.at[src]).wait()
    wide[...] = qkv_recv[...].reshape(32 * 3 * HALF, 128).astype(F32)

    def gather(source, first, stride):
        return jnp.concatenate(
            [source[pl.ds(first + r, 32, stride=stride), :] for r in range(RES)], axis=0
        ).astype(BF16)

    for s in range(SEQ_RUN // 2):
        lanes = slice(s * 128, s * 128 + 128)
        for j, keep in enumerate((q_all, k_all, v_all)):
            keep[:, lanes] = gather(wide, j * HALF + s * RES, 3 * HALF)
    part[:, 0] = rows_dot(q_all[...], k_all[...], NT).reshape(8, 16, 128)

    wait_bytes(g_recv.at[:, pl.ds(0, 3)], g_recv_sem)
    own_g.wait()
    wide_g[...] = g_recv[...].reshape(32 * HALF, 128).astype(F32)
    for s in range(SEQ_RUN // 2):
        g_all[:, s * 128 : s * 128 + 128] = gather(wide_g, s * RES, HALF)
    part[:, 1] = rows_dot(g_all[...], v_all[...], NT).reshape(8, 16, 128)

    def send_part(k, _):
        to = (z + k) % 8
        pltpu.make_async_remote_copy(
            part.at[to], part_recv.at[z], part_send_sem, part_recv_sem,
            device_id=z_peer(to), device_id_type=MESH,
        ).start()
        return 0

    lax.fori_loop(1, 8, send_part, 0)
    part_recv[z] = part[z]
    wait_bytes(part_recv.at[pl.ds(0, 7)], part_recv_sem)
    total[...] = jnp.sum(part_recv[...], axis=0)

    def send_total(k, _):
        to = (w + k) % 8
        pltpu.make_async_remote_copy(
            total, total_recv.at[w], total_send_sem, total_recv_sem,
            device_id=line_peer(to), device_id_type=MESH,
        ).start()
        return 0

    lax.fori_loop(1, 8, send_total, 0)
    total_recv[w] = total[...]
    wait_bytes(total_recv.at[pl.ds(0, 7)], total_recv_sem)
    sums = jnp.sum(total_recv[...], axis=0)
    scores, prob_grad = scale * sums[0], sums[1]
    grown = jnp.exp(scores - jnp.max(scores, axis=-1, keepdims=True))
    probability = grown / jnp.sum(grown, axis=-1, keepdims=True)
    row_total = jnp.sum(probability * prob_grad, axis=-1, keepdims=True)
    probs[z, 0] = (scale * probability * (prob_grad - row_total)).astype(BF16)
    probs[z, 1] = probability.astype(BF16)

    def send_probs(k, _):
        to = (z + k) % 8
        pltpu.make_async_remote_copy(
            probs.at[z], probs.at[z], probs_send_sem, probs_recv_sem,
            device_id=z_peer(to), device_id_type=MESH,
        ).start()
        return 0

    lax.fori_loop(1, 8, send_probs, 0)
    wait_bytes(probs.at[pl.ds(0, 7)], probs_recv_sem)
    score_grad = probs[:, 0].reshape(128, 128)
    prob_low = probs[:, 1].reshape(128, 128)

    for j, grad in enumerate(
        (
            rows_dot(score_grad, k_all[...]),
            rows_dot(score_grad, q_all[...], TN),
            rows_dot(prob_low, g_all[...], TN),
        )
    ):
        for s in range(SEQ_RUN // 2):
            for r in range(RES):
                wide[pl.ds(j * HALF + s * RES + r, 32, stride=3 * HALF), :] = grad[
                    r * 32 : r * 32 + 32, s * 128 : s * 128 + 128
                ]
    back_send[...] = wide[...].astype(BF16).reshape(8, 4, 3 * HALF, 128)

    def place(k):
        back = 3 - k
        return (yh + back + back // 2 - 2 * (back // 3)) % 4

    def send_back(k, _):
        src = place(k)

        def one(j, _):
            to = (g + j) % 8
            pltpu.make_async_remote_copy(
                back_send.at[to, src], back_recv.at[g, src], back_send_sem, back_recv_sem.at[src],
                device_id=head_peer(to), device_id_type=MESH,
            ).start()
            return 0

        lax.fori_loop(1, 8, one, 0)
        pltpu.make_async_copy(back_send.at[g, src], back_recv.at[g, src], back_own_sem.at[src]).start()
        return 0

    lax.fori_loop(0, 4, send_back, 0)

    low_back = lax.broadcasted_iota(jnp.int32, (3 * HALF, 128), 1) < HEAD_DIM

    def out_copy(to, slot):
        return pltpu.make_async_remote_copy(
            out_send.at[to], out.at[run(slot)], out_send_sem, out_recv_sem.at[slot],
            device_id=y_peer(to), device_id_type=MESH,
        )

    def finish(src):
        wait_bytes(back_recv.at[pl.ds(0, 7), src], back_recv_sem.at[src])
        pltpu.make_async_copy(back_send.at[g, src], back_recv.at[g, src], back_own_sem.at[src]).wait()
        tops, bottoms = [], []
        for p in range(4):
            a, b = back_recv[2 * p, src], back_recv[2 * p + 1, src]
            tops.append(jnp.where(low_back, a, b))
            bottoms.append(pltpu.roll(jnp.where(low_back, b, a), HEAD_DIM, 1))
        top, bottom = jnp.concatenate(tops, axis=1), jnp.concatenate(bottoms, axis=1)
        grad = None
        for j, weight in enumerate((wq, wk, wv)):
            rows = slice(j * HALF, (j + 1) * HALF)
            term = rows_dot(jnp.concatenate([top[rows], bottom[rows]], axis=0), weight[...], NT)
            grad = term if grad is None else grad + term
        out_send[src] = grad.astype(BF16).reshape(SEQ_RUN, RES, D)

    def finish_far(k, _):
        src = place(k)
        finish(src)
        out_copy(src, yh).start()
        return 0

    lax.fori_loop(0, 3, finish_far, 0)
    finish(yh)
    own_out = pltpu.make_async_copy(out_send.at[yh], out.at[run(yh)], out_own_sem)
    own_out.start()

    wait_bytes(g_own.at[pl.ds(0, 7)], near_send_sem)
    wait_bytes(g_own.at[:, pl.ds(0, 3)], g_send_sem)
    wait_bytes(qkv_send.at[pl.ds(0, 7)], qkv_send_sem)
    wait_bytes(part_recv.at[pl.ds(0, 7)], part_send_sem)
    wait_bytes(total_recv.at[pl.ds(0, 7)], total_send_sem)
    wait_bytes(probs.at[pl.ds(0, 7)], probs_send_sem)
    wait_bytes(back_send.at[pl.ds(0, 7)], back_send_sem)
    wait_bytes(out_send.at[pl.ds(0, 3)], out_send_sem)

    def wait_out(k, _):
        src = (yh + k) % 4
        out_copy(src, src).wait_recv()
        return 0

    lax.fori_loop(1, 4, wait_out, 0)
    own_out.wait()


def body(activations, out_grad, w_query, w_key, w_value, w_output):
    seqs_total = activations.shape[0] * lax.axis_size("seq")
    scale = 1.0 / math.sqrt(HEAD_DIM * seqs_total)
    hbm = pl.BlockSpec(memory_space=pltpu.HBM)
    dma = pltpu.SemaphoreType.DMA
    vmem = pltpu.VMEM
    return pl.pallas_call(
        lambda *refs: kernel(scale, *refs),
        out_shape=jax.ShapeDtypeStruct(activations.shape, BF16),
        in_specs=[hbm] * 6,
        out_specs=pl.BlockSpec(memory_space=pl.ANY),
        scratch_shapes=[
            vmem((D, FEATURES), BF16),
            vmem((D, FEATURES), BF16),
            vmem((D, FEATURES), BF16),
            vmem((FEATURES, D), BF16),
            vmem((4 * SEQ_RUN, RES, D), BF16),
            vmem((4, SEQ_RUN, RES, D), BF16),
            vmem((8, 4, HALF, 128), BF16),
            vmem((8, 4, HALF, 128), BF16),
            vmem((8, 4, HALF, 128), BF16),
            vmem((8, 4, 3 * HALF, 128), BF16),
            vmem((8, 4, 3 * HALF, 128), BF16),
            vmem((32 * 3 * HALF, 128), F32),
            vmem((32 * HALF, 128), F32),
            vmem((128, SEQ_RUN * HEAD_DIM), BF16),
            vmem((128, SEQ_RUN * HEAD_DIM), BF16),
            vmem((128, SEQ_RUN * HEAD_DIM), BF16),
            vmem((128, SEQ_RUN * HEAD_DIM), BF16),
            vmem((8, 2, 16, 128), F32),
            vmem((8, 2, 16, 128), F32),
            vmem((2, 16, 128), F32),
            vmem((8, 2, 16, 128), F32),
            vmem((8, 2, 16, 128), BF16),
            vmem((8, 4, 3 * HALF, 128), BF16),
            vmem((8, 4, 3 * HALF, 128), BF16),
            vmem((4, SEQ_RUN, RES, D), BF16),
            dma((6,)), dma((4,)), dma((4,)), dma, dma, dma,
            dma, dma, dma, dma, dma, dma((4,)),
            dma, dma, dma, dma,
            dma, dma, dma, dma((4,)), dma((4,)),
            dma, dma((4,)), dma,
        ],
        compiler_params=pltpu.CompilerParams(
            collective_id=0, has_side_effects=True, vmem_limit_bytes=54 * 2**20
        ),
        cost_estimate=pl.CostEstimate(
            flops=2 * 10**9, bytes_accessed=5 * 10**6, transcendentals=2048
        ),
    )(activations, out_grad, w_query, w_key, w_value, w_output)


def solution(mesh):
    rows = P("seq", "res", None)
    return jax.shard_map(
        body,
        mesh=mesh,
        in_specs=(rows, rows, P(), P(), P(), P()),
        out_specs=rows,
        check_vma=False,
    )
```

```python
import math

import jax
import jax.numpy as jnp
from jax import lax
from jax.experimental import pallas as pl
from jax.experimental.pallas import tpu as pltpu
from jax.sharding import PartitionSpec as P

MESH = pl.DeviceIdType.MESH
F32, BF16 = jnp.float32, jnp.bfloat16
D = 768
FEATURES = 512
HEAD_DIM = 64
SEQ_RUN = 16
RES = 4
ROWS = SEQ_RUN * RES
HALF = ROWS // 2
NT = (((1,), (1,)), ((), ()))
TN = (((0,), (0,)), ((), ()))


def rows_dot(a, b, dims=(((1,), (0,)), ((), ()))):
    return lax.dot_general(a, b, dims, preferred_element_type=F32)


def kernel(
    scale,
    act, og, wq_hbm, wk_hbm, wv_hbm, wo_hbm,
    out,
    wq, wk, wv, wo, og_v, xr, g_near, g_own, g_recv, qkv_send, qkv_recv,
    wide, wide_g, q_all, k_all, v_all, g_all, grads,
    part, part_recv, total, total_recv, probs, back_send, back_recv, out_send,
    load_sem, x_send_sem, x_recv_sem, near_send_sem, near_recv_sem, near_own_sem,
    g_send_sem, g_recv_sem, g_own_sem, qkv_send_sem, qkv_recv_sem, qkv_own_sem,
    part_send_sem, part_recv_sem, total_send_sem, total_recv_sem,
    probs_send_sem, probs_recv_sem, back_send_sem, back_recv_sem, back_own_sem,
    out_send_sem, out_recv_sem, out_own_sem,
):
    seq, res = lax.axis_index("seq"), lax.axis_index("res")
    ylo, z = seq // 8, seq % 8
    x, yh, core = res // 8, (res // 2) % 4, res % 2
    g = x * 2 + core
    w = yh * 2 + ylo

    def y_peer(h):
        return (seq, x * 8 + h * 2 + core)

    def head_peer(h):
        return (seq, (h // 2) * 8 + yh * 2 + h % 2)

    def z_peer(k):
        return (ylo * 8 + k, res)

    def line_peer(k):
        return ((k % 2) * 8 + z, x * 8 + (k // 2) * 2 + core)

    def run(h):
        return pl.ds(pl.multiple_of(h * SEQ_RUN, SEQ_RUN), SEQ_RUN)

    def wait_bytes(ref, sem):
        pltpu.make_async_copy(ref, ref, sem).wait()

    loads = [
        pltpu.make_async_copy(og, og_v, load_sem.at[0]),
        pltpu.make_async_copy(wo_hbm, wo, load_sem.at[1]),
        pltpu.make_async_copy(act.at[run(yh)], xr.at[yh], load_sem.at[2]),
        pltpu.make_async_copy(wq_hbm, wq, load_sem.at[3]),
        pltpu.make_async_copy(wk_hbm, wk, load_sem.at[4]),
        pltpu.make_async_copy(wv_hbm, wv, load_sem.at[5]),
    ]
    for load in loads:
        load.start()

    barrier = pltpu.get_barrier_semaphore()

    def greet(k, _):
        pl.semaphore_signal(barrier, inc=1, device_id=head_peer((g + k) % 8), device_id_type=MESH)
        pl.semaphore_signal(barrier, inc=1, device_id=z_peer((z + k) % 8), device_id_type=MESH)
        pl.semaphore_signal(barrier, inc=1, device_id=line_peer((w + k) % 8), device_id_type=MESH)
        return 0

    lax.fori_loop(1, 8, greet, 0)

    pl.semaphore_wait(barrier, 21)

    def x_copy(to, slot):
        return pltpu.make_async_remote_copy(
            act.at[run(to)], xr.at[slot], x_send_sem.at[to], x_recv_sem.at[slot],
            device_id=y_peer(to), device_id_type=MESH,
        )

    after, before, far = (yh + 1) % 4, (yh + 3) % 4, (yh + 2) % 4
    x_copy(after, yh).start()
    x_copy(before, yh).start()

    low = lax.broadcasted_iota(jnp.int32, (HALF, 128), 1) < HEAD_DIM

    def fold(top, bottom):
        turned = pltpu.roll(bottom, HEAD_DIM, 1)
        return jnp.where(low, top, turned), jnp.where(low, turned, top)

    loads[0].wait()
    loads[1].wait()
    grad_rows = rows_dot(og_v[...].reshape(4 * ROWS, D), wo[...], NT).astype(BF16)
    for c in range(4):
        for p in range(4):
            pair = grad_rows[c * ROWS : (c + 1) * ROWS, p * 128 : p * 128 + 128]
            g_near[2 * p, c], g_near[2 * p + 1, c] = fold(pair[:HALF], pair[HALF:])

    def near_first(k):
        return k + k // 2 - 2 * (k // 3)

    def send_near(k, _):
        to = (g + k) % 8
        pltpu.make_async_remote_copy(
            g_near.at[to], g_own.at[g], near_send_sem, near_recv_sem,
            device_id=head_peer(to), device_id_type=MESH,
        ).start()
        return 0

    lax.fori_loop(1, 8, send_near, 0)
    near_copy = pltpu.make_async_copy(g_near.at[g], g_own.at[g], near_own_sem)
    near_copy.start()
    x_copy(far, yh).start()

    def do_qkv(src):
        rows = xr[src].reshape(ROWS, D)
        for j, weight in enumerate((wq, wk, wv)):
            a = rows_dot(rows, weight[...]).astype(BF16)
            for p in range(4):
                pair = a[:, p * 128 : p * 128 + 128]
                even, odd = fold(pair[:HALF], pair[HALF:])
                qkv_send[src, 2 * p, j * HALF : (j + 1) * HALF] = even
                qkv_send[src, 2 * p + 1, j * HALF : (j + 1) * HALF] = odd

        def one(k, _):
            to = (g + k) % 8
            pltpu.make_async_remote_copy(
                qkv_send.at[src, to], qkv_recv.at[src, g], qkv_send_sem, qkv_recv_sem.at[src],
                device_id=head_peer(to), device_id_type=MESH,
            ).start()
            return 0

        lax.fori_loop(1, 8, one, 0)
        pltpu.make_async_copy(qkv_send.at[src, g], qkv_recv.at[src, g], qkv_own_sem.at[src]).start()

    for load in loads[2:]:
        load.wait()
    do_qkv(yh)

    def g_copy(to, slot):
        return pltpu.make_async_remote_copy(
            g_own.at[:, to], g_recv.at[slot], g_send_sem, g_recv_sem.at[slot],
            device_id=y_peer(to), device_id_type=MESH,
        )

    def near_qkv(k, _):
        src = (yh + 1 + 2 * k) % 4
        x_copy(src, src).wait_recv()
        do_qkv(src)

        @pl.when(k == 0)
        def _():
            wait_bytes(g_own.at[pl.ds(0, 7)], near_recv_sem)
            near_copy.wait()
            g_copy(after, yh).start()
            g_copy(before, yh).start()
            g_copy(far, yh).start()

        return 0

    lax.fori_loop(0, 2, near_qkv, 0)
    own_g = pltpu.make_async_copy(g_own.at[:, yh], g_recv.at[yh], g_own_sem)
    own_g.start()

    def gather(source, first, stride):
        return jnp.concatenate(
            [source[pl.ds(first + r, 8, stride=stride), :] for r in range(RES)], axis=0
        ).astype(BF16)

    def chunk(src):
        return pl.ds(pl.multiple_of(src * 32, 32), 32)

    def take_qkv(src):
        wait_bytes(qkv_recv.at[src, pl.ds(0, 7)], qkv_recv_sem.at[src])
        pltpu.make_async_copy(qkv_send.at[src, g], qkv_recv.at[src, g], qkv_own_sem.at[src]).wait()
        wide[...] = qkv_recv[src].reshape(8 * 3 * HALF, 128).astype(F32)
        for s in range(SEQ_RUN // 2):
            for j, keep in enumerate((q_all, k_all, v_all)):
                keep[chunk(src), s * 128 : s * 128 + 128] = gather(wide, j * HALF + s * RES, 3 * HALF)

    def take_g(src):
        wide_g[...] = g_recv[src].reshape(8 * HALF, 128).astype(F32)
        for s in range(SEQ_RUN // 2):
            g_all[chunk(src), s * 128 : s * 128 + 128] = gather(wide_g, s * RES, HALF)

    take_qkv(yh)
    own_g.wait()
    take_g(yh)

    x_copy(far, far).wait_recv()
    do_qkv(far)

    def next_qkv(k, _):
        take_qkv((yh + near_first(k)) % 4)
        return 0

    lax.fori_loop(1, 4, next_qkv, 0)
    part[:, 0] = rows_dot(q_all[...], k_all[...], NT).reshape(8, 16, 128)

    def next_g(k, _):
        src = (yh + near_first(k)) % 4
        g_copy(src, src).wait_recv()
        take_g(src)
        return 0

    lax.fori_loop(1, 4, next_g, 0)
    part[:, 1] = rows_dot(g_all[...], v_all[...], NT).reshape(8, 16, 128)

    def send_part(k, _):
        to = (z + k) % 8
        pltpu.make_async_remote_copy(
            part.at[to], part_recv.at[z], part_send_sem, part_recv_sem,
            device_id=z_peer(to), device_id_type=MESH,
        ).start()
        return 0

    lax.fori_loop(1, 8, send_part, 0)
    part_recv[z] = part[z]
    wait_bytes(part_recv.at[pl.ds(0, 7)], part_recv_sem)
    total[...] = jnp.sum(part_recv[...], axis=0)

    def send_total(k, _):
        to = (w + k) % 8
        pltpu.make_async_remote_copy(
            total, total_recv.at[w], total_send_sem, total_recv_sem,
            device_id=line_peer(to), device_id_type=MESH,
        ).start()
        return 0

    lax.fori_loop(1, 8, send_total, 0)
    total_recv[w] = total[...]
    wait_bytes(total_recv.at[pl.ds(0, 7)], total_recv_sem)
    sums = jnp.sum(total_recv[...], axis=0)
    scores, prob_grad = scale * sums[0], sums[1]
    grown = jnp.exp(scores - jnp.max(scores, axis=-1, keepdims=True))
    probability = grown / jnp.sum(grown, axis=-1, keepdims=True)
    row_total = jnp.sum(probability * prob_grad, axis=-1, keepdims=True)
    probs[z, 0] = (scale * probability * (prob_grad - row_total)).astype(BF16)
    probs[z, 1] = probability.astype(BF16)

    def send_probs(k, _):
        to = (z + k) % 8
        pltpu.make_async_remote_copy(
            probs.at[z], probs.at[z], probs_send_sem, probs_recv_sem,
            device_id=z_peer(to), device_id_type=MESH,
        ).start()
        return 0

    lax.fori_loop(1, 8, send_probs, 0)
    wait_bytes(probs.at[pl.ds(0, 7)], probs_recv_sem)
    score_grad = probs[:, 0].reshape(128, 128)
    prob_low = probs[:, 1].reshape(128, 128)

    grads[0] = rows_dot(score_grad, k_all[...])
    grads[1] = rows_dot(score_grad, q_all[...], TN)
    grads[2] = rows_dot(prob_low, g_all[...], TN)

    def place(k):
        return (yh + near_first(3 - k)) % 4

    def send_back(k, _):
        src = place(k)
        for j in range(3):
            for s in range(SEQ_RUN // 2):
                for r in range(RES):
                    rows = pl.ds(pl.multiple_of(src * 32 + r * 8, 8), 8)
                    wide[pl.ds(j * HALF + s * RES + r, 8, stride=3 * HALF), :] = grads[
                        j, rows, s * 128 : s * 128 + 128
                    ]
        back_send[src] = wide[...].astype(BF16).reshape(8, 3 * HALF, 128)

        def one(j, _):
            to = (g + j) % 8
            pltpu.make_async_remote_copy(
                back_send.at[src, to], back_recv.at[src, g], back_send_sem, back_recv_sem.at[src],
                device_id=head_peer(to), device_id_type=MESH,
            ).start()
            return 0

        lax.fori_loop(1, 8, one, 0)
        pltpu.make_async_copy(back_send.at[src, g], back_recv.at[src, g], back_own_sem.at[src]).start()
        return 0

    lax.fori_loop(0, 4, send_back, 0)

    low_back = lax.broadcasted_iota(jnp.int32, (3 * HALF, 128), 1) < HEAD_DIM

    def out_copy(to, slot, n):
        return pltpu.make_async_remote_copy(
            out_send.at[to, n], out.at[run(slot), :, pl.ds(n * (D // 2), D // 2)], out_send_sem, out_recv_sem.at[slot, n],
            device_id=y_peer(to), device_id_type=MESH,
        )

    def finish(src, remote):
        wait_bytes(back_recv.at[src, pl.ds(0, 7)], back_recv_sem.at[src])
        pltpu.make_async_copy(back_send.at[src, g], back_recv.at[src, g], back_own_sem.at[src]).wait()
        tops, bottoms = [], []
        for p in range(4):
            a, b = back_recv[src, 2 * p], back_recv[src, 2 * p + 1]
            tops.append(jnp.where(low_back, a, b))
            bottoms.append(pltpu.roll(jnp.where(low_back, b, a), HEAD_DIM, 1))
        top, bottom = jnp.concatenate(tops, axis=1), jnp.concatenate(bottoms, axis=1)
        sides = [
            jnp.concatenate([top[j * HALF : (j + 1) * HALF], bottom[j * HALF : (j + 1) * HALF]], axis=0)
            for j in range(3)
        ]
        for n in range(2):
            cols = slice(n * (D // 2), (n + 1) * (D // 2))
            grad = None
            for side, weight in zip(sides, (wq, wk, wv)):
                term = rows_dot(side, weight[cols, :], NT)
                grad = term if grad is None else grad + term
            out_send[src, n] = grad.astype(BF16).reshape(SEQ_RUN, RES, D // 2)
            if remote:
                out_copy(src, yh, n).start()

    def finish_far(k, _):
        src = place(k)
        finish(src, True)
        return 0

    lax.fori_loop(0, 3, finish_far, 0)
    finish(yh, False)
    own_outs = [
        pltpu.make_async_copy(out_send.at[yh, n], out.at[run(yh), :, pl.ds(n * (D // 2), D // 2)], out_own_sem.at[n])
        for n in range(2)
    ]
    for own_out in own_outs:
        own_out.start()

    wait_bytes(g_own.at[pl.ds(0, 7)], near_send_sem)
    for to in (after, before, far):
        x_copy(to, yh).wait_send()
    wait_bytes(g_recv.at[pl.ds(0, 3)], g_send_sem)
    wait_bytes(qkv_send.at[:, pl.ds(0, 7)], qkv_send_sem)
    wait_bytes(part_recv.at[pl.ds(0, 7)], part_send_sem)
    wait_bytes(total_recv.at[pl.ds(0, 7)], total_send_sem)
    wait_bytes(probs.at[pl.ds(0, 7)], probs_send_sem)
    wait_bytes(back_send.at[:, pl.ds(0, 7)], back_send_sem)
    wait_bytes(out_send.at[pl.ds(0, 3)], out_send_sem)

    def wait_out(k, _):
        src = (yh + k) % 4
        for n in range(2):
            out_copy(src, src, n).wait_recv()
        return 0

    lax.fori_loop(1, 4, wait_out, 0)
    for own_out in own_outs:
        own_out.wait()


def body(activations, out_grad, w_query, w_key, w_value, w_output):
    seqs_total = activations.shape[0] * lax.axis_size("seq")
    scale = 1.0 / math.sqrt(HEAD_DIM * seqs_total)
    hbm = pl.BlockSpec(memory_space=pltpu.HBM)
    dma = pltpu.SemaphoreType.DMA
    vmem = pltpu.VMEM
    return pl.pallas_call(
        lambda *refs: kernel(scale, *refs),
        out_shape=jax.ShapeDtypeStruct(activations.shape, BF16),
        in_specs=[hbm] * 6,
        out_specs=pl.BlockSpec(memory_space=pl.ANY),
        scratch_shapes=[
            vmem((D, FEATURES), BF16),
            vmem((D, FEATURES), BF16),
            vmem((D, FEATURES), BF16),
            vmem((FEATURES, D), BF16),
            vmem((4 * SEQ_RUN, RES, D), BF16),
            vmem((4, SEQ_RUN, RES, D), BF16),
            vmem((8, 4, HALF, 128), BF16),
            vmem((8, 4, HALF, 128), BF16),
            vmem((4, 8, HALF, 128), BF16),
            vmem((4, 8, 3 * HALF, 128), BF16),
            vmem((4, 8, 3 * HALF, 128), BF16),
            vmem((8 * 3 * HALF, 128), F32),
            vmem((8 * HALF, 128), F32),
            vmem((128, SEQ_RUN * HEAD_DIM), BF16),
            vmem((128, SEQ_RUN * HEAD_DIM), BF16),
            vmem((128, SEQ_RUN * HEAD_DIM), BF16),
            vmem((128, SEQ_RUN * HEAD_DIM), BF16),
            vmem((3, 128, SEQ_RUN * HEAD_DIM), F32),
            vmem((8, 2, 16, 128), F32),
            vmem((8, 2, 16, 128), F32),
            vmem((2, 16, 128), F32),
            vmem((8, 2, 16, 128), F32),
            vmem((8, 2, 16, 128), BF16),
            vmem((4, 8, 3 * HALF, 128), BF16),
            vmem((4, 8, 3 * HALF, 128), BF16),
            vmem((4, 2, SEQ_RUN, RES, D // 2), BF16),
            dma((6,)), dma((4,)), dma((4,)), dma, dma, dma,
            dma, dma((4,)), dma, dma, dma((4,)), dma((4,)),
            dma, dma, dma, dma,
            dma, dma, dma, dma((4,)), dma((4,)),
            dma, dma((4, 2)), dma((2,)),
        ],
        compiler_params=pltpu.CompilerParams(
            collective_id=0, has_side_effects=True, vmem_limit_bytes=54784 * 2**10
        ),
        cost_estimate=pl.CostEstimate(
            flops=2 * 10**9, bytes_accessed=5 * 10**6, transcendentals=2048
        ),
    )(activations, out_grad, w_query, w_key, w_value, w_output)


def solution(mesh):
    rows = P("seq", "res", None)
    return jax.shard_map(
        body,
        mesh=mesh,
        in_specs=(rows, rows, P(), P(), P(), P()),
        out_specs=rows,
        check_vma=False,
    )
```

```python
import math

import jax
import jax.numpy as jnp
from jax import lax
from jax.experimental import pallas as pl
from jax.experimental.pallas import tpu as pltpu
from jax.sharding import PartitionSpec as P

MESH = pl.DeviceIdType.MESH
F32, BF16 = jnp.float32, jnp.bfloat16
D = 768
FEATURES = 512
HEAD_DIM = 64
SEQ_RUN = 16
RES = 4
ROWS = SEQ_RUN * RES
HALF = ROWS // 2
QUARTER = SEQ_RUN // 4
PART = HALF // 2
NT = (((1,), (1,)), ((), ()))
TN = (((0,), (0,)), ((), ()))


def rows_dot(a, b, dims=(((1,), (0,)), ((), ()))):
    return lax.dot_general(a, b, dims, preferred_element_type=F32)


def kernel(
    scale,
    act, og, wq_hbm, wk_hbm, wv_hbm, wo_hbm,
    out,
    wq, wk, wv, wo, og_v, xr, g_near, g_own, g_recv, qkv_send, qkv_recv,
    wide, wide_g, q_all, k_all, v_all, g_all, grads,
    part, part_recv, total, total_recv, probs, wide_back, back_send, back_recv, early, late, out_send,
    load_sem, x_send_sem, x_recv_sem, near_send_sem, near_recv_sem, near_own_sem,
    g_send_sem, g_recv_sem, g_own_sem, qkv_send_sem, qkv_recv_sem, qkv_own_sem,
    part_send_sem, part_recv_sem, total_send_sem, total_recv_sem,
    probs_send_sem, probs_recv_sem, back_send_sem, back_recv_sem, back_own_sem,
    early_send_sem, early_recv_sem, late_send_sem, late_recv_sem, late_own_sem,
    out_send_sem, out_recv_sem, out_own_sem,
):
    seq, res = lax.axis_index("seq"), lax.axis_index("res")
    ylo, z = seq // 8, seq % 8
    x, yh, core = res // 8, (res // 2) % 4, res % 2
    g = x * 2 + core
    w = yh * 2 + ylo

    def y_peer(h):
        return (seq, x * 8 + h * 2 + core)

    def head_peer(h):
        return (seq, (h // 2) * 8 + yh * 2 + h % 2)

    def z_peer(k):
        return (ylo * 8 + k, res)

    def line_peer(k):
        return ((k % 2) * 8 + z, x * 8 + (k // 2) * 2 + core)

    def run(h):
        return pl.ds(pl.multiple_of(h * SEQ_RUN, SEQ_RUN), SEQ_RUN)

    def wait_bytes(ref, sem):
        pltpu.make_async_copy(ref, ref, sem).wait()

    loads = [
        pltpu.make_async_copy(og, og_v, load_sem.at[0]),
        pltpu.make_async_copy(wo_hbm, wo, load_sem.at[1]),
        pltpu.make_async_copy(act.at[run(yh)], xr.at[yh], load_sem.at[2]),
        pltpu.make_async_copy(wq_hbm, wq, load_sem.at[3]),
        pltpu.make_async_copy(wk_hbm, wk, load_sem.at[4]),
        pltpu.make_async_copy(wv_hbm, wv, load_sem.at[5]),
    ]
    for load in loads:
        load.start()

    barrier = pltpu.get_barrier_semaphore()

    def greet(k, _):
        pl.semaphore_signal(barrier, inc=1, device_id=head_peer((g + k) % 8), device_id_type=MESH)
        pl.semaphore_signal(barrier, inc=1, device_id=z_peer((z + k) % 8), device_id_type=MESH)
        pl.semaphore_signal(barrier, inc=1, device_id=line_peer((w + k) % 8), device_id_type=MESH)
        return 0

    lax.fori_loop(1, 8, greet, 0)

    pl.semaphore_wait(barrier, 21)

    def x_copy(to, slot):
        return pltpu.make_async_remote_copy(
            act.at[run(to)], xr.at[slot], x_send_sem.at[to], x_recv_sem.at[slot],
            device_id=y_peer(to), device_id_type=MESH,
        )

    after, before, far = (yh + 1) % 4, (yh + 3) % 4, (yh + 2) % 4
    x_copy(after, yh).start()
    x_copy(before, yh).start()

    low = lax.broadcasted_iota(jnp.int32, (HALF, 128), 1) < HEAD_DIM

    def fold(top, bottom):
        turned = pltpu.roll(bottom, HEAD_DIM, 1)
        return jnp.where(low, top, turned), jnp.where(low, turned, top)

    loads[0].wait()
    loads[1].wait()
    grad_rows = rows_dot(og_v[...].reshape(4 * ROWS, D), wo[...], NT).astype(BF16)
    for c in range(4):
        for p in range(4):
            pair = grad_rows[c * ROWS : (c + 1) * ROWS, p * 128 : p * 128 + 128]
            g_near[2 * p, c], g_near[2 * p + 1, c] = fold(pair[:HALF], pair[HALF:])

    def near_first(k):
        return k + k // 2 - 2 * (k // 3)

    def send_near(k, _):
        to = (g + k) % 8
        pltpu.make_async_remote_copy(
            g_near.at[to], g_own.at[g], near_send_sem, near_recv_sem,
            device_id=head_peer(to), device_id_type=MESH,
        ).start()
        return 0

    lax.fori_loop(1, 8, send_near, 0)
    near_copy = pltpu.make_async_copy(g_near.at[g], g_own.at[g], near_own_sem)
    near_copy.start()
    x_copy(far, yh).start()

    def do_qkv(src):
        rows = xr[src].reshape(ROWS, D)
        for j, weight in enumerate((wq, wk, wv)):
            a = rows_dot(rows, weight[...]).astype(BF16)
            for p in range(4):
                pair = a[:, p * 128 : p * 128 + 128]
                even, odd = fold(pair[:HALF], pair[HALF:])
                qkv_send[src, 2 * p, j * HALF : (j + 1) * HALF] = even
                qkv_send[src, 2 * p + 1, j * HALF : (j + 1) * HALF] = odd

        def one(k, _):
            to = (g + k) % 8
            pltpu.make_async_remote_copy(
                qkv_send.at[src, to], qkv_recv.at[src, g], qkv_send_sem, qkv_recv_sem.at[src],
                device_id=head_peer(to), device_id_type=MESH,
            ).start()
            return 0

        lax.fori_loop(1, 8, one, 0)
        pltpu.make_async_copy(qkv_send.at[src, g], qkv_recv.at[src, g], qkv_own_sem.at[src]).start()

    for load in loads[2:]:
        load.wait()
    do_qkv(yh)

    def g_copy(to, slot):
        return pltpu.make_async_remote_copy(
            g_own.at[:, to], g_recv.at[slot], g_send_sem, g_recv_sem.at[slot],
            device_id=y_peer(to), device_id_type=MESH,
        )

    def near_qkv(k, _):
        src = (yh + 1 + 2 * k) % 4
        x_copy(src, src).wait_recv()
        do_qkv(src)

        @pl.when(k == 0)
        def _():
            wait_bytes(g_own.at[pl.ds(0, 7)], near_recv_sem)
            near_copy.wait()
            g_copy(after, yh).start()
            g_copy(before, yh).start()
            g_copy(far, yh).start()

        return 0

    lax.fori_loop(0, 2, near_qkv, 0)
    own_g = pltpu.make_async_copy(g_own.at[:, yh], g_recv.at[yh], g_own_sem)
    own_g.start()

    def gather(source, first, stride):
        return jnp.concatenate(
            [source[pl.ds(first + r, 8, stride=stride), :] for r in range(RES)], axis=0
        ).astype(BF16)

    def chunk(src):
        return pl.ds(pl.multiple_of(src * 32, 32), 32)

    def take_qkv(src):
        wait_bytes(qkv_recv.at[src, pl.ds(0, 7)], qkv_recv_sem.at[src])
        pltpu.make_async_copy(qkv_send.at[src, g], qkv_recv.at[src, g], qkv_own_sem.at[src]).wait()
        wide[...] = qkv_recv[src].reshape(8 * 3 * HALF, 128).astype(F32)
        for s in range(SEQ_RUN // 2):
            for j, keep in enumerate((q_all, k_all, v_all)):
                keep[chunk(src), s * 128 : s * 128 + 128] = gather(wide, j * HALF + s * RES, 3 * HALF)

    def take_g(src):
        wide_g[...] = g_recv[src].reshape(8 * HALF, 128).astype(F32)
        for s in range(SEQ_RUN // 2):
            g_all[chunk(src), s * 128 : s * 128 + 128] = gather(wide_g, s * RES, HALF)

    take_qkv(yh)
    own_g.wait()
    take_g(yh)

    x_copy(far, far).wait_recv()
    do_qkv(far)

    def next_qkv(k, _):
        take_qkv((yh + near_first(k)) % 4)
        return 0

    lax.fori_loop(1, 4, next_qkv, 0)
    part[:, 0] = rows_dot(q_all[...], k_all[...], NT).reshape(8, 16, 128)

    def next_g(k, _):
        src = (yh + near_first(k)) % 4
        g_copy(src, src).wait_recv()
        take_g(src)
        return 0

    lax.fori_loop(1, 4, next_g, 0)
    part[:, 1] = rows_dot(g_all[...], v_all[...], NT).reshape(8, 16, 128)

    def send_part(k, _):
        to = (z + k) % 8
        pltpu.make_async_remote_copy(
            part.at[to], part_recv.at[z], part_send_sem, part_recv_sem,
            device_id=z_peer(to), device_id_type=MESH,
        ).start()
        return 0

    lax.fori_loop(1, 8, send_part, 0)
    part_recv[z] = part[z]
    wait_bytes(part_recv.at[pl.ds(0, 7)], part_recv_sem)
    total[...] = jnp.sum(part_recv[...], axis=0)

    def send_total(k, _):
        to = (w + k) % 8
        pltpu.make_async_remote_copy(
            total, total_recv.at[w], total_send_sem, total_recv_sem,
            device_id=line_peer(to), device_id_type=MESH,
        ).start()
        return 0

    lax.fori_loop(1, 8, send_total, 0)
    total_recv[w] = total[...]
    wait_bytes(total_recv.at[pl.ds(0, 7)], total_recv_sem)
    sums = jnp.sum(total_recv[...], axis=0)
    scores, prob_grad = scale * sums[0], sums[1]
    grown = jnp.exp(scores - jnp.max(scores, axis=-1, keepdims=True))
    probability = grown / jnp.sum(grown, axis=-1, keepdims=True)
    row_total = jnp.sum(probability * prob_grad, axis=-1, keepdims=True)
    probs[z, 0] = (scale * probability * (prob_grad - row_total)).astype(BF16)
    probs[z, 1] = probability.astype(BF16)

    def send_probs(k, _):
        to = (z + k) % 8
        pltpu.make_async_remote_copy(
            probs.at[z], probs.at[z], probs_send_sem, probs_recv_sem,
            device_id=z_peer(to), device_id_type=MESH,
        ).start()
        return 0

    lax.fori_loop(1, 8, send_probs, 0)
    wait_bytes(probs.at[pl.ds(0, 7)], probs_recv_sem)
    score_grad = probs[:, 0].reshape(128, 128)
    prob_low = probs[:, 1].reshape(128, 128)

    grads[0] = rows_dot(score_grad, k_all[...])
    grads[1] = rows_dot(score_grad, q_all[...], TN)
    grads[2] = rows_dot(prob_low, g_all[...], TN)

    def unit(k):
        return (yh + 2 - k // 2 + 2 * (k // 3)) % 4, (k + 3) // 4

    def pack(src, h):
        for j in range(3):
            for n in range(QUARTER):
                lanes = (h * QUARTER + n) * 128
                for r in range(RES):
                    rows = pl.ds(pl.multiple_of(src * 32 + r * 8, 8), 8)
                    wide_back[pl.ds(j * PART + n * RES + r, 8, stride=3 * PART), :] = grads[
                        j, rows, lanes : lanes + 128
                    ]
        back_send[src, h] = wide_back[...].astype(BF16).reshape(8, 3 * PART, 128)

    def send_back(src, h):
        def one(k, _):
            to = (g + k) % 8
            pltpu.make_async_remote_copy(
                back_send.at[src, h, to], back_recv.at[src, h, g],
                back_send_sem.at[src, h], back_recv_sem.at[src, h],
                device_id=head_peer(to), device_id_type=MESH,
            ).start()
            return 0

        lax.fori_loop(1, 8, one, 0)
        pltpu.make_async_copy(
            back_send.at[src, h, g], back_recv.at[src, h, g], back_own_sem.at[src, h]
        ).start()

    def early_copy(to, slot):
        return pltpu.make_async_remote_copy(
            back_send.at[to, 0], early.at[slot], early_send_sem.at[to], early_recv_sem.at[slot],
            device_id=y_peer(to), device_id_type=MESH,
        )

    def send_early(k, _):
        src = (yh + 1 + 2 * k) % 4
        pack(src, 0)
        early_copy(src, yh).start()
        return 0

    lax.fori_loop(0, 2, send_early, 0)
    pack(far, 0)
    send_back(far, 0)

    def send_second(k, _):
        src = unit(k)[0]
        pack(src, 1)
        send_back(src, 1)
        return 0

    lax.fori_loop(1, 4, send_second, 0)
    pack(yh, 0)
    send_back(yh, 0)
    pack(yh, 1)
    send_back(yh, 1)

    low_back = lax.broadcasted_iota(jnp.int32, (3 * PART, 128), 1) < HEAD_DIM

    def unfold(block):
        tops, bottoms = [], []
        for p in range(4):
            a, b = block(2 * p), block(2 * p + 1)
            tops.append(jnp.where(low_back, a, b))
            bottoms.append(pltpu.roll(jnp.where(low_back, b, a), HEAD_DIM, 1))
        top, bottom = jnp.concatenate(tops, axis=1), jnp.concatenate(bottoms, axis=1)
        return [
            jnp.concatenate([top[j * PART : (j + 1) * PART], bottom[j * PART : (j + 1) * PART]], axis=0)
            for j in range(3)
        ]

    def finish(sides, columns, keep):
        grad = None
        for side, weight in zip(sides, (wq, wk, wv)):
            term = rows_dot(side, weight[columns * (D // 2) : (columns + 1) * (D // 2), :], NT)
            grad = term if grad is None else grad + term
        pieces = grad.astype(BF16).reshape(-1, 2, QUARTER, RES, D // 2)
        for n in range(pieces.shape[0]):
            out_send[keep + n, columns] = pieces[n]

    def place(run_at, h, columns, piece):
        start = pl.multiple_of(run_at * SEQ_RUN, SEQ_RUN) + h * QUARTER + piece * (SEQ_RUN // 2)
        return out.at[pl.ds(start, QUARTER), :, pl.ds(columns * (D // 2), D // 2)]

    def arrived(src, h):
        wait_bytes(back_recv.at[src, h, pl.ds(0, 7)], back_recv_sem.at[src, h])
        pltpu.make_async_copy(
            back_send.at[src, h, g], back_recv.at[src, h, g], back_own_sem.at[src, h]
        ).wait()
        return unfold(lambda head: back_recv[src, h, head])

    def finish_unit(k, _):
        src, h = unit(k)
        sides = arrived(src, h)
        for columns in range(2):
            finish(sides, columns, k)
            for piece in range(2):
                pltpu.make_async_remote_copy(
                    out_send.at[k, columns, piece], place(yh, h, columns, piece),
                    out_send_sem.at[k], out_recv_sem.at[yh],
                    device_id=y_peer(src), device_id_type=MESH,
                ).start()

        @pl.when(k == 1)
        def _():
            def forward(n, _):
                slot = (yh + 1 + 2 * n) % 4
                early_copy(slot, slot).wait_recv()

                def one(k, _):
                    to = (g + k) % 8
                    pltpu.make_async_remote_copy(
                        early.at[slot, to], late.at[slot, g], late_send_sem.at[slot], late_recv_sem.at[slot],
                        device_id=head_peer(to), device_id_type=MESH,
                    ).start()
                    return 0

                lax.fori_loop(1, 8, one, 0)
                pltpu.make_async_copy(early.at[slot, g], late.at[slot, g], late_own_sem.at[slot]).start()
                return 0

            lax.fori_loop(0, 2, forward, 0)

        return 0

    lax.fori_loop(0, 4, finish_unit, 0)

    def both(one, two):
        return [jnp.concatenate(pair, axis=0) for pair in zip(one, two)]

    own_outs = []

    def finish_here(sides, keep, runs):
        for columns in range(2):
            finish(sides, columns, keep)
            for n, (run_at, h) in enumerate(runs):
                for piece in range(2):
                    copy = pltpu.make_async_copy(
                        out_send.at[keep + n, columns, piece], place(run_at, h, columns, piece),
                        out_own_sem.at[len(own_outs)],
                    )
                    copy.start()
                    own_outs.append(copy)

    finish_here(both(arrived(yh, 0), arrived(yh, 1)), 4, ((yh, 0), (yh, 1)))

    def arrived_late(slot):
        wait_bytes(late.at[slot, pl.ds(0, 7)], late_recv_sem.at[slot])
        pltpu.make_async_copy(early.at[slot, g], late.at[slot, g], late_own_sem.at[slot]).wait()
        return unfold(lambda head: late[slot, head])

    finish_here(both(arrived_late(after), arrived_late(before)), 6, ((after, 0), (before, 0)))

    wait_bytes(g_own.at[pl.ds(0, 7)], near_send_sem)
    for to in (after, before, far):
        x_copy(to, yh).wait_send()
    wait_bytes(g_recv.at[pl.ds(0, 3)], g_send_sem)
    wait_bytes(qkv_send.at[:, pl.ds(0, 7)], qkv_send_sem)
    wait_bytes(part_recv.at[pl.ds(0, 7)], part_send_sem)
    wait_bytes(total_recv.at[pl.ds(0, 7)], total_send_sem)
    wait_bytes(probs.at[pl.ds(0, 7)], probs_send_sem)
    def wait_back(k, _):
        src, h = unit(k)
        wait_bytes(back_send.at[src, h, pl.ds(0, 7)], back_send_sem.at[src, h])
        wait_bytes(out_send.at[k], out_send_sem.at[k])
        return 0

    lax.fori_loop(0, 4, wait_back, 0)
    for h in range(2):
        wait_bytes(back_send.at[yh, h, pl.ds(0, 7)], back_send_sem.at[yh, h])
    for slot in (after, before):
        early_copy(slot, yh).wait_send()
        wait_bytes(late.at[slot, pl.ds(0, 7)], late_send_sem.at[slot])
    wait_bytes(out.at[pl.ds(0, SEQ_RUN)], out_recv_sem.at[far])
    for slot in (after, before):
        wait_bytes(out.at[pl.ds(0, SEQ_RUN // 2)], out_recv_sem.at[slot])
    for own_out in own_outs:
        own_out.wait()


def body(activations, out_grad, w_query, w_key, w_value, w_output):
    seqs_total = activations.shape[0] * lax.axis_size("seq")
    scale = 1.0 / math.sqrt(HEAD_DIM * seqs_total)
    hbm = pl.BlockSpec(memory_space=pltpu.HBM)
    dma = pltpu.SemaphoreType.DMA
    vmem = pltpu.VMEM
    return pl.pallas_call(
        lambda *refs: kernel(scale, *refs),
        out_shape=jax.ShapeDtypeStruct(activations.shape, BF16),
        in_specs=[hbm] * 6,
        out_specs=pl.BlockSpec(memory_space=pl.ANY),
        scratch_shapes=[
            vmem((D, FEATURES), BF16),
            vmem((D, FEATURES), BF16),
            vmem((D, FEATURES), BF16),
            vmem((FEATURES, D), BF16),
            vmem((4 * SEQ_RUN, RES, D), BF16),
            vmem((4, SEQ_RUN, RES, D), BF16),
            vmem((8, 4, HALF, 128), BF16),
            vmem((8, 4, HALF, 128), BF16),
            vmem((4, 8, HALF, 128), BF16),
            vmem((4, 8, 3 * HALF, 128), BF16),
            vmem((4, 8, 3 * HALF, 128), BF16),
            vmem((8 * 3 * HALF, 128), F32),
            vmem((8 * HALF, 128), F32),
            vmem((128, SEQ_RUN * HEAD_DIM), BF16),
            vmem((128, SEQ_RUN * HEAD_DIM), BF16),
            vmem((128, SEQ_RUN * HEAD_DIM), BF16),
            vmem((128, SEQ_RUN * HEAD_DIM), BF16),
            vmem((3, 128, SEQ_RUN * HEAD_DIM), F32),
            vmem((8, 2, 16, 128), F32),
            vmem((8, 2, 16, 128), F32),
            vmem((2, 16, 128), F32),
            vmem((8, 2, 16, 128), F32),
            vmem((8, 2, 16, 128), BF16),
            vmem((8 * 3 * PART, 128), F32),
            vmem((4, 2, 8, 3 * PART, 128), BF16),
            vmem((4, 2, 8, 3 * PART, 128), BF16),
            vmem((4, 8, 3 * PART, 128), BF16),
            vmem((4, 8, 3 * PART, 128), BF16),
            vmem((8, 2, 2, QUARTER, RES, D // 2), BF16),
            dma((6,)), dma((4,)), dma((4,)), dma, dma, dma,
            dma, dma((4,)), dma, dma, dma((4,)), dma((4,)),
            dma, dma, dma, dma,
            dma, dma, dma((4, 2)), dma((4, 2)), dma((4, 2)),
            dma((4,)), dma((4,)), dma((4,)), dma((4,)), dma((4,)),
            dma((4,)), dma((4,)), dma((16,)),
        ],
        compiler_params=pltpu.CompilerParams(
            collective_id=0, has_side_effects=True, vmem_limit_bytes=54784 * 2**10
        ),
        cost_estimate=pl.CostEstimate(
            flops=2 * 10**9, bytes_accessed=5 * 10**6, transcendentals=2048
        ),
    )(activations, out_grad, w_query, w_key, w_value, w_output)


def solution(mesh):
    rows = P("seq", "res", None)
    return jax.shard_map(
        body,
        mesh=mesh,
        in_specs=(rows, rows, P(), P(), P(), P()),
        out_specs=rows,
        check_vma=False,
    )
```

```python
import math

import jax
import jax.numpy as jnp
from jax import lax
from jax.experimental import pallas as pl
from jax.experimental.pallas import tpu as pltpu
from jax.sharding import PartitionSpec as P

MESH = pl.DeviceIdType.MESH
F32, BF16 = jnp.float32, jnp.bfloat16
D = 768
FEATURES = 512
HEAD_DIM = 64
SEQ_RUN = 16
RES = 4
ROWS = SEQ_RUN * RES
HALF = ROWS // 2
QUARTER = SEQ_RUN // 4
PART = HALF // 2
NT = (((1,), (1,)), ((), ()))
TN = (((0,), (0,)), ((), ()))


def rows_dot(a, b, dims=(((1,), (0,)), ((), ()))):
    return lax.dot_general(a, b, dims, preferred_element_type=F32)


def kernel(
    scale,
    act, og, wq_hbm, wk_hbm, wv_hbm, wo_hbm,
    out,
    wq, wk, wv, wo, og_v, xr, g_near, g_own, g_recv, qkv_send, qkv_recv,
    wide, wide_g, q_all, k_all, v_all, g_all, grads,
    part, part_recv, total, total_recv, probs, wide_back, back_send, back_recv, early, late, out_send,
    load_sem, x_send_sem, x_recv_sem, near_send_sem, near_recv_sem, near_own_sem,
    g_send_sem, g_recv_sem, g_own_sem, qkv_send_sem, qkv_recv_sem, qkv_own_sem,
    part_send_sem, part_recv_sem, total_send_sem, total_recv_sem,
    probs_send_sem, probs_recv_sem, back_send_sem, back_recv_sem, back_own_sem,
    early_send_sem, early_recv_sem, late_send_sem, late_recv_sem, late_own_sem,
    out_send_sem, out_recv_sem, out_own_sem,
):
    seq, res = lax.axis_index("seq"), lax.axis_index("res")
    ylo, z = seq // 8, seq % 8
    x, yh, core = res // 8, (res // 2) % 4, res % 2
    g = x * 2 + core
    w = yh * 2 + ylo

    def y_peer(h):
        return (seq, x * 8 + h * 2 + core)

    def head_peer(h):
        return (seq, (h // 2) * 8 + yh * 2 + h % 2)

    def z_peer(k):
        return (ylo * 8 + k, res)

    def line_peer(k):
        return ((k % 2) * 8 + z, x * 8 + (k // 2) * 2 + core)

    def run(h):
        return pl.ds(pl.multiple_of(h * SEQ_RUN, SEQ_RUN), SEQ_RUN)

    def wait_bytes(ref, sem):
        pltpu.make_async_copy(ref, ref, sem).wait()

    loads = [
        pltpu.make_async_copy(og, og_v, load_sem.at[0]),
        pltpu.make_async_copy(wo_hbm, wo, load_sem.at[1]),
        pltpu.make_async_copy(act.at[run(yh)], xr.at[yh], load_sem.at[2]),
        pltpu.make_async_copy(wq_hbm, wq, load_sem.at[3]),
        pltpu.make_async_copy(wk_hbm, wk, load_sem.at[4]),
        pltpu.make_async_copy(wv_hbm, wv, load_sem.at[5]),
    ]
    for load in loads:
        load.start()

    barrier = pltpu.get_barrier_semaphore()

    def greet(k, _):
        pl.semaphore_signal(barrier, inc=1, device_id=head_peer((g + k) % 8), device_id_type=MESH)
        pl.semaphore_signal(barrier, inc=1, device_id=z_peer((z + k) % 8), device_id_type=MESH)
        pl.semaphore_signal(barrier, inc=1, device_id=line_peer((w + k) % 8), device_id_type=MESH)
        return 0

    lax.fori_loop(1, 8, greet, 0)

    pl.semaphore_wait(barrier, 21)

    def x_copy(to, slot):
        return pltpu.make_async_remote_copy(
            act.at[run(to)], xr.at[slot], x_send_sem.at[to], x_recv_sem.at[slot],
            device_id=y_peer(to), device_id_type=MESH,
        )

    after, before, far = (yh + 1) % 4, (yh + 3) % 4, (yh + 2) % 4
    x_copy(after, yh).start()
    x_copy(before, yh).start()

    low = lax.broadcasted_iota(jnp.int32, (HALF, 128), 1) < HEAD_DIM

    def fold(top, bottom):
        turned = pltpu.roll(bottom, HEAD_DIM, 1)
        return jnp.where(low, top, turned), jnp.where(low, turned, top)

    loads[0].wait()
    loads[1].wait()
    grad_rows = rows_dot(og_v[...].reshape(4 * ROWS, D), wo[...], NT).astype(BF16)
    for c in range(4):
        for p in range(4):
            pair = grad_rows[c * ROWS : (c + 1) * ROWS, p * 128 : p * 128 + 128]
            g_near[2 * p, c], g_near[2 * p + 1, c] = fold(pair[:HALF], pair[HALF:])

    def near_first(k):
        return k + k // 2 - 2 * (k // 3)

    def send_near(k, _):
        to = (g + k) % 8
        pltpu.make_async_remote_copy(
            g_near.at[to], g_own.at[g], near_send_sem, near_recv_sem,
            device_id=head_peer(to), device_id_type=MESH,
        ).start()
        return 0

    lax.fori_loop(1, 8, send_near, 0)
    near_copy = pltpu.make_async_copy(g_near.at[g], g_own.at[g], near_own_sem)
    near_copy.start()
    x_copy(far, yh).start()

    def do_qkv(src):
        rows = xr[src].reshape(ROWS, D)
        for j, weight in enumerate((wq, wk, wv)):
            a = rows_dot(rows, weight[...]).astype(BF16)
            for p in range(4):
                pair = a[:, p * 128 : p * 128 + 128]
                even, odd = fold(pair[:HALF], pair[HALF:])
                qkv_send[src, 2 * p, j * HALF : (j + 1) * HALF] = even
                qkv_send[src, 2 * p + 1, j * HALF : (j + 1) * HALF] = odd

        def one(k, _):
            to = (g + k) % 8
            pltpu.make_async_remote_copy(
                qkv_send.at[src, to], qkv_recv.at[src, g], qkv_send_sem, qkv_recv_sem.at[src],
                device_id=head_peer(to), device_id_type=MESH,
            ).start()
            return 0

        lax.fori_loop(1, 8, one, 0)
        pltpu.make_async_copy(qkv_send.at[src, g], qkv_recv.at[src, g], qkv_own_sem.at[src]).start()

    for load in loads[2:]:
        load.wait()
    do_qkv(yh)

    def g_copy(to, slot):
        return pltpu.make_async_remote_copy(
            g_own.at[:, to], g_recv.at[slot], g_send_sem, g_recv_sem.at[slot],
            device_id=y_peer(to), device_id_type=MESH,
        )

    def near_qkv(k, _):
        src = (yh + 1 + 2 * k) % 4
        x_copy(src, src).wait_recv()
        do_qkv(src)

        @pl.when(k == 0)
        def _():
            wait_bytes(g_own.at[pl.ds(0, 7)], near_recv_sem)
            near_copy.wait()
            g_copy(after, yh).start()
            g_copy(before, yh).start()
            g_copy(far, yh).start()

        return 0

    lax.fori_loop(0, 2, near_qkv, 0)
    own_g = pltpu.make_async_copy(g_own.at[:, yh], g_recv.at[yh], g_own_sem)
    own_g.start()

    def gather(source, first, stride):
        return jnp.concatenate(
            [source[pl.ds(first + r, 8, stride=stride), :] for r in range(RES)], axis=0
        ).astype(BF16)

    def chunk(src):
        return pl.ds(pl.multiple_of(src * 32, 32), 32)

    def take_qkv(src):
        wait_bytes(qkv_recv.at[src, pl.ds(0, 7)], qkv_recv_sem.at[src])
        pltpu.make_async_copy(qkv_send.at[src, g], qkv_recv.at[src, g], qkv_own_sem.at[src]).wait()
        wide[...] = qkv_recv[src].reshape(8 * 3 * HALF, 128).astype(F32)
        for s in range(SEQ_RUN // 2):
            for j, keep in enumerate((q_all, k_all, v_all)):
                keep[chunk(src), s * 128 : s * 128 + 128] = gather(wide, j * HALF + s * RES, 3 * HALF)

    def take_g(src):
        wide_g[...] = g_recv[src].reshape(8 * HALF, 128).astype(F32)
        for s in range(SEQ_RUN // 2):
            g_all[chunk(src), s * 128 : s * 128 + 128] = gather(wide_g, s * RES, HALF)

    take_qkv(yh)
    own_g.wait()
    take_g(yh)

    x_copy(far, far).wait_recv()
    do_qkv(far)

    def next_g(k, _):
        src = (yh + near_first(k)) % 4
        g_copy(src, src).wait_recv()
        take_g(src)
        return 0

    lax.fori_loop(1, 4, next_g, 0)

    def next_qkv(k, _):
        take_qkv((yh + near_first(k)) % 4)
        return 0

    lax.fori_loop(1, 4, next_qkv, 0)

    def send_part(n, product):
        part[n] = product.reshape(8, 16, 128)

        def one(k, _):
            to = (z + k) % 8
            pltpu.make_async_remote_copy(
                part.at[n, to], part_recv.at[n, z], part_send_sem.at[n], part_recv_sem.at[n],
                device_id=z_peer(to), device_id_type=MESH,
            ).start()
            return 0

        lax.fori_loop(1, 8, one, 0)
        part_recv[n, z] = part[n, z]

    def send_total(n):
        wait_bytes(part_recv.at[n, pl.ds(0, 7)], part_recv_sem.at[n])
        total[n] = jnp.sum(part_recv[n], axis=0)

        def one(k, _):
            to = (w + k) % 8
            pltpu.make_async_remote_copy(
                total.at[n], total_recv.at[n, w], total_send_sem.at[n], total_recv_sem.at[n],
                device_id=line_peer(to), device_id_type=MESH,
            ).start()
            return 0

        lax.fori_loop(1, 8, one, 0)
        total_recv[n, w] = total[n]

    def whole(n):
        wait_bytes(total_recv.at[n, pl.ds(0, 7)], total_recv_sem.at[n])
        return jnp.sum(total_recv[n], axis=0)

    send_part(0, rows_dot(q_all[...], k_all[...], NT))
    send_part(1, rows_dot(g_all[...], v_all[...], NT))
    send_total(0)
    send_total(1)
    scores = scale * whole(0)
    grown = jnp.exp(scores - jnp.max(scores, axis=-1, keepdims=True))
    probability = grown / jnp.sum(grown, axis=-1, keepdims=True)
    prob_grad = whole(1)
    row_total = jnp.sum(probability * prob_grad, axis=-1, keepdims=True)
    probs[z, 0] = (scale * probability * (prob_grad - row_total)).astype(BF16)
    probs[z, 1] = probability.astype(BF16)

    def send_probs(k, _):
        to = (z + k) % 8
        pltpu.make_async_remote_copy(
            probs.at[z], probs.at[z], probs_send_sem, probs_recv_sem,
            device_id=z_peer(to), device_id_type=MESH,
        ).start()
        return 0

    lax.fori_loop(1, 8, send_probs, 0)
    wait_bytes(probs.at[pl.ds(0, 7)], probs_recv_sem)
    score_grad = probs[:, 0].reshape(128, 128)
    prob_low = probs[:, 1].reshape(128, 128)

    grads[0] = rows_dot(score_grad, k_all[...])
    grads[1] = rows_dot(score_grad, q_all[...], TN)
    grads[2] = rows_dot(prob_low, g_all[...], TN)

    def unit(k):
        return (yh + 2 - k // 2 + 2 * (k // 3)) % 4, (k + 3) // 4

    def pack(src, h):
        for j in range(3):
            for n in range(QUARTER):
                lanes = (h * QUARTER + n) * 128
                for r in range(RES):
                    rows = pl.ds(pl.multiple_of(src * 32 + r * 8, 8), 8)
                    wide_back[pl.ds(j * PART + n * RES + r, 8, stride=3 * PART), :] = grads[
                        j, rows, lanes : lanes + 128
                    ]
        back_send[src, h] = wide_back[...].astype(BF16).reshape(8, 3 * PART, 128)

    def send_back(src, h):
        def one(k, _):
            to = (g + k) % 8
            pltpu.make_async_remote_copy(
                back_send.at[src, h, to], back_recv.at[src, h, g],
                back_send_sem.at[src, h], back_recv_sem.at[src, h],
                device_id=head_peer(to), device_id_type=MESH,
            ).start()
            return 0

        lax.fori_loop(1, 8, one, 0)
        pltpu.make_async_copy(
            back_send.at[src, h, g], back_recv.at[src, h, g], back_own_sem.at[src, h]
        ).start()

    def early_copy(to, slot):
        return pltpu.make_async_remote_copy(
            back_send.at[to, 0], early.at[slot], early_send_sem.at[to], early_recv_sem.at[slot],
            device_id=y_peer(to), device_id_type=MESH,
        )

    def send_early(k, _):
        src = (yh + 1 + 2 * k) % 4
        pack(src, 0)
        early_copy(src, yh).start()
        return 0

    lax.fori_loop(0, 2, send_early, 0)
    pack(far, 0)
    send_back(far, 0)

    def send_second(k, _):
        src = unit(k)[0]
        pack(src, 1)
        send_back(src, 1)
        return 0

    lax.fori_loop(1, 4, send_second, 0)
    pack(yh, 0)
    send_back(yh, 0)
    pack(yh, 1)
    send_back(yh, 1)

    low_back = lax.broadcasted_iota(jnp.int32, (3 * PART, 128), 1) < HEAD_DIM

    def unfold(block):
        tops, bottoms = [], []
        for p in range(4):
            a, b = block(2 * p), block(2 * p + 1)
            tops.append(jnp.where(low_back, a, b))
            bottoms.append(pltpu.roll(jnp.where(low_back, b, a), HEAD_DIM, 1))
        top, bottom = jnp.concatenate(tops, axis=1), jnp.concatenate(bottoms, axis=1)
        return [
            jnp.concatenate([top[j * PART : (j + 1) * PART], bottom[j * PART : (j + 1) * PART]], axis=0)
            for j in range(3)
        ]

    def finish(sides, columns, keep):
        grad = None
        for side, weight in zip(sides, (wq, wk, wv)):
            term = rows_dot(side, weight[columns * (D // 2) : (columns + 1) * (D // 2), :], NT)
            grad = term if grad is None else grad + term
        pieces = grad.astype(BF16).reshape(-1, 2, QUARTER, RES, D // 2)
        for n in range(pieces.shape[0]):
            out_send[keep + n, columns] = pieces[n]

    def place(run_at, h, columns, piece):
        start = pl.multiple_of(run_at * SEQ_RUN, SEQ_RUN) + h * QUARTER + piece * (SEQ_RUN // 2)
        return out.at[pl.ds(start, QUARTER), :, pl.ds(columns * (D // 2), D // 2)]

    def arrived(src, h):
        wait_bytes(back_recv.at[src, h, pl.ds(0, 7)], back_recv_sem.at[src, h])
        pltpu.make_async_copy(
            back_send.at[src, h, g], back_recv.at[src, h, g], back_own_sem.at[src, h]
        ).wait()
        return unfold(lambda head: back_recv[src, h, head])

    def finish_unit(k, _):
        src, h = unit(k)
        sides = arrived(src, h)
        for columns in range(2):
            finish(sides, columns, k)
            for piece in range(2):
                pltpu.make_async_remote_copy(
                    out_send.at[k, columns, piece], place(yh, h, columns, piece),
                    out_send_sem.at[k], out_recv_sem.at[yh],
                    device_id=y_peer(src), device_id_type=MESH,
                ).start()

        @pl.when(k == 1)
        def _():
            def forward(n, _):
                slot = (yh + 1 + 2 * n) % 4
                early_copy(slot, slot).wait_recv()

                def one(k, _):
                    to = (g + k) % 8
                    pltpu.make_async_remote_copy(
                        early.at[slot, to], late.at[slot, g], late_send_sem.at[slot], late_recv_sem.at[slot],
                        device_id=head_peer(to), device_id_type=MESH,
                    ).start()
                    return 0

                lax.fori_loop(1, 8, one, 0)
                pltpu.make_async_copy(early.at[slot, g], late.at[slot, g], late_own_sem.at[slot]).start()
                return 0

            lax.fori_loop(0, 2, forward, 0)

        return 0

    lax.fori_loop(0, 4, finish_unit, 0)

    def both(one, two):
        return [jnp.concatenate(pair, axis=0) for pair in zip(one, two)]

    own_outs = []

    def finish_here(sides, keep, runs):
        for columns in range(2):
            finish(sides, columns, keep)
            for n, (run_at, h) in enumerate(runs):
                for piece in range(2):
                    copy = pltpu.make_async_copy(
                        out_send.at[keep + n, columns, piece], place(run_at, h, columns, piece),
                        out_own_sem.at[len(own_outs)],
                    )
                    copy.start()
                    own_outs.append(copy)

    finish_here(both(arrived(yh, 0), arrived(yh, 1)), 4, ((yh, 0), (yh, 1)))

    def arrived_late(slot):
        wait_bytes(late.at[slot, pl.ds(0, 7)], late_recv_sem.at[slot])
        pltpu.make_async_copy(early.at[slot, g], late.at[slot, g], late_own_sem.at[slot]).wait()
        return unfold(lambda head: late[slot, head])

    finish_here(both(arrived_late(after), arrived_late(before)), 6, ((after, 0), (before, 0)))

    wait_bytes(g_own.at[pl.ds(0, 7)], near_send_sem)
    for to in (after, before, far):
        x_copy(to, yh).wait_send()
    wait_bytes(g_recv.at[pl.ds(0, 3)], g_send_sem)
    wait_bytes(qkv_send.at[:, pl.ds(0, 7)], qkv_send_sem)
    for n in range(2):
        wait_bytes(part_recv.at[n, pl.ds(0, 7)], part_send_sem.at[n])
        wait_bytes(total_recv.at[n, pl.ds(0, 7)], total_send_sem.at[n])
    wait_bytes(probs.at[pl.ds(0, 7)], probs_send_sem)
    def wait_back(k, _):
        src, h = unit(k)
        wait_bytes(back_send.at[src, h, pl.ds(0, 7)], back_send_sem.at[src, h])
        wait_bytes(out_send.at[k], out_send_sem.at[k])
        return 0

    lax.fori_loop(0, 4, wait_back, 0)
    for h in range(2):
        wait_bytes(back_send.at[yh, h, pl.ds(0, 7)], back_send_sem.at[yh, h])
    for slot in (after, before):
        early_copy(slot, yh).wait_send()
        wait_bytes(late.at[slot, pl.ds(0, 7)], late_send_sem.at[slot])
    wait_bytes(out.at[pl.ds(0, SEQ_RUN)], out_recv_sem.at[far])
    for slot in (after, before):
        wait_bytes(out.at[pl.ds(0, SEQ_RUN // 2)], out_recv_sem.at[slot])
    for own_out in own_outs:
        own_out.wait()


def body(activations, out_grad, w_query, w_key, w_value, w_output):
    seqs_total = activations.shape[0] * lax.axis_size("seq")
    scale = 1.0 / math.sqrt(HEAD_DIM * seqs_total)
    hbm = pl.BlockSpec(memory_space=pltpu.HBM)
    dma = pltpu.SemaphoreType.DMA
    vmem = pltpu.VMEM
    return pl.pallas_call(
        lambda *refs: kernel(scale, *refs),
        out_shape=jax.ShapeDtypeStruct(activations.shape, BF16),
        in_specs=[hbm] * 6,
        out_specs=pl.BlockSpec(memory_space=pl.ANY),
        scratch_shapes=[
            vmem((D, FEATURES), BF16),
            vmem((D, FEATURES), BF16),
            vmem((D, FEATURES), BF16),
            vmem((FEATURES, D), BF16),
            vmem((4 * SEQ_RUN, RES, D), BF16),
            vmem((4, SEQ_RUN, RES, D), BF16),
            vmem((8, 4, HALF, 128), BF16),
            vmem((8, 4, HALF, 128), BF16),
            vmem((4, 8, HALF, 128), BF16),
            vmem((4, 8, 3 * HALF, 128), BF16),
            vmem((4, 8, 3 * HALF, 128), BF16),
            vmem((8 * 3 * HALF, 128), F32),
            vmem((8 * HALF, 128), F32),
            vmem((128, SEQ_RUN * HEAD_DIM), BF16),
            vmem((128, SEQ_RUN * HEAD_DIM), BF16),
            vmem((128, SEQ_RUN * HEAD_DIM), BF16),
            vmem((128, SEQ_RUN * HEAD_DIM), BF16),
            vmem((3, 128, SEQ_RUN * HEAD_DIM), F32),
            vmem((2, 8, 16, 128), F32),
            vmem((2, 8, 16, 128), F32),
            vmem((2, 16, 128), F32),
            vmem((2, 8, 16, 128), F32),
            vmem((8, 2, 16, 128), BF16),
            vmem((8 * 3 * PART, 128), F32),
            vmem((4, 2, 8, 3 * PART, 128), BF16),
            vmem((4, 2, 8, 3 * PART, 128), BF16),
            vmem((4, 8, 3 * PART, 128), BF16),
            vmem((4, 8, 3 * PART, 128), BF16),
            vmem((8, 2, 2, QUARTER, RES, D // 2), BF16),
            dma((6,)), dma((4,)), dma((4,)), dma, dma, dma,
            dma, dma((4,)), dma, dma, dma((4,)), dma((4,)),
            dma((2,)), dma((2,)), dma((2,)), dma((2,)),
            dma, dma, dma((4, 2)), dma((4, 2)), dma((4, 2)),
            dma((4,)), dma((4,)), dma((4,)), dma((4,)), dma((4,)),
            dma((4,)), dma((4,)), dma((16,)),
        ],
        compiler_params=pltpu.CompilerParams(
            collective_id=0, has_side_effects=True, vmem_limit_bytes=54784 * 2**10
        ),
        cost_estimate=pl.CostEstimate(
            flops=2 * 10**9, bytes_accessed=5 * 10**6, transcendentals=2048
        ),
    )(activations, out_grad, w_query, w_key, w_value, w_output)


def solution(mesh):
    rows = P("seq", "res", None)
    return jax.shard_map(
        body,
        mesh=mesh,
        in_specs=(rows, rows, P(), P(), P(), P()),
        out_specs=rows,
        check_vma=False,
    )
```

```python
import math

import jax
import jax.numpy as jnp
from jax import lax
from jax.experimental import pallas as pl
from jax.experimental.pallas import tpu as pltpu
from jax.sharding import PartitionSpec as P

MESH = pl.DeviceIdType.MESH
F32, BF16 = jnp.float32, jnp.bfloat16
D = 768
FEATURES = 512
HEAD_DIM = 64
SEQ_RUN = 16
RES = 4
ROWS = SEQ_RUN * RES
HALF = ROWS // 2
QUARTER = SEQ_RUN // 4
PART = HALF // 2
NT = (((1,), (1,)), ((), ()))
TN = (((0,), (0,)), ((), ()))


def rows_dot(a, b, dims=(((1,), (0,)), ((), ()))):
    return lax.dot_general(a, b, dims, preferred_element_type=F32)


def kernel(
    scale,
    act, og, wq_hbm, wk_hbm, wv_hbm, wo_hbm,
    out,
    wq, wk, wv, wo, og_v, xr, g_near, g_own, g_recv, qkv_send, qkv_recv,
    wide, wide_g, q_all, k_all, v_all, g_all, grads,
    part, part_recv, total, total_recv, probs, wide_back, back_send, back_recv, early, late, out_send,
    load_sem, x_send_sem, x_recv_sem, near_send_sem, near_recv_sem, near_own_sem,
    g_send_sem, g_recv_sem, g_own_sem, qkv_send_sem, qkv_recv_sem, qkv_own_sem,
    part_send_sem, part_recv_sem, total_send_sem, total_recv_sem,
    probs_send_sem, probs_recv_sem, back_send_sem, back_recv_sem, back_own_sem,
    early_send_sem, early_recv_sem, late_send_sem, late_recv_sem, late_own_sem,
    out_send_sem, out_recv_sem, out_own_sem,
):
    seq, res = lax.axis_index("seq"), lax.axis_index("res")
    ylo, z = seq // 8, seq % 8
    x, yh, core = res // 8, (res // 2) % 4, res % 2
    g = x * 2 + core
    w = yh * 2 + ylo

    def y_peer(h):
        return (seq, x * 8 + h * 2 + core)

    def head_peer(h):
        return (seq, (h // 2) * 8 + yh * 2 + h % 2)

    def z_peer(k):
        return (ylo * 8 + k, res)

    def line_peer(k):
        return ((k % 2) * 8 + z, x * 8 + (k // 2) * 2 + core)

    def run(h):
        return pl.ds(pl.multiple_of(h * SEQ_RUN, SEQ_RUN), SEQ_RUN)

    def wait_bytes(ref, sem):
        pltpu.make_async_copy(ref, ref, sem).wait()

    loads = [
        pltpu.make_async_copy(og, og_v, load_sem.at[0]),
        pltpu.make_async_copy(wo_hbm, wo, load_sem.at[1]),
        pltpu.make_async_copy(act.at[run(yh)], xr.at[yh], load_sem.at[2]),
        pltpu.make_async_copy(wq_hbm, wq, load_sem.at[3]),
        pltpu.make_async_copy(wk_hbm, wk, load_sem.at[4]),
        pltpu.make_async_copy(wv_hbm, wv, load_sem.at[5]),
    ]
    for load in loads:
        load.start()

    barrier = pltpu.get_barrier_semaphore()

    def greet(k, _):
        pl.semaphore_signal(barrier, inc=1, device_id=head_peer((g + k) % 8), device_id_type=MESH)
        pl.semaphore_signal(barrier, inc=1, device_id=z_peer((z + k) % 8), device_id_type=MESH)
        pl.semaphore_signal(barrier, inc=1, device_id=line_peer((w + k) % 8), device_id_type=MESH)
        return 0

    lax.fori_loop(1, 8, greet, 0)

    pl.semaphore_wait(barrier, 21)

    def x_copy(to, slot):
        return pltpu.make_async_remote_copy(
            act.at[run(to)], xr.at[slot], x_send_sem.at[to], x_recv_sem.at[slot],
            device_id=y_peer(to), device_id_type=MESH,
        )

    after, before, far = (yh + 1) % 4, (yh + 3) % 4, (yh + 2) % 4
    x_copy(after, yh).start()
    x_copy(before, yh).start()

    low = lax.broadcasted_iota(jnp.int32, (HALF, 128), 1) < HEAD_DIM

    def fold(top, bottom):
        turned = pltpu.roll(bottom, HEAD_DIM, 1)
        return jnp.where(low, top, turned), jnp.where(low, turned, top)

    loads[0].wait()
    loads[1].wait()
    grad_rows = rows_dot(og_v[...].reshape(4 * ROWS, D), wo[...], NT).astype(BF16)
    for c in range(4):
        for p in range(4):
            pair = grad_rows[c * ROWS : (c + 1) * ROWS, p * 128 : p * 128 + 128]
            g_near[2 * p, c], g_near[2 * p + 1, c] = fold(pair[:HALF], pair[HALF:])

    def near_first(k):
        return k + k // 2 - 2 * (k // 3)

    def send_near(k, _):
        to = (g + k) % 8
        pltpu.make_async_remote_copy(
            g_near.at[to], g_own.at[g], near_send_sem, near_recv_sem,
            device_id=head_peer(to), device_id_type=MESH,
        ).start()
        return 0

    lax.fori_loop(1, 8, send_near, 0)
    near_copy = pltpu.make_async_copy(g_near.at[g], g_own.at[g], near_own_sem)
    near_copy.start()
    x_copy(far, yh).start()

    def do_qkv(src):
        rows = xr[src].reshape(ROWS, D)
        for j, weight in enumerate((wq, wk, wv)):
            a = rows_dot(rows, weight[...]).astype(BF16)
            for p in range(4):
                pair = a[:, p * 128 : p * 128 + 128]
                even, odd = fold(pair[:HALF], pair[HALF:])
                qkv_send[src, 2 * p, j * HALF : (j + 1) * HALF] = even
                qkv_send[src, 2 * p + 1, j * HALF : (j + 1) * HALF] = odd

        def one(k, _):
            to = (g + k) % 8
            pltpu.make_async_remote_copy(
                qkv_send.at[src, to], qkv_recv.at[src, g], qkv_send_sem, qkv_recv_sem.at[src],
                device_id=head_peer(to), device_id_type=MESH,
            ).start()
            return 0

        lax.fori_loop(1, 8, one, 0)
        pltpu.make_async_copy(qkv_send.at[src, g], qkv_recv.at[src, g], qkv_own_sem.at[src]).start()

    for load in loads[2:]:
        load.wait()
    do_qkv(yh)

    def g_copy(to, slot):
        return pltpu.make_async_remote_copy(
            g_own.at[:, to], g_recv.at[slot], g_send_sem, g_recv_sem.at[slot],
            device_id=y_peer(to), device_id_type=MESH,
        )

    def near_qkv(k, _):
        src = (yh + 1 + 2 * k) % 4
        x_copy(src, src).wait_recv()
        do_qkv(src)

        @pl.when(k == 0)
        def _():
            wait_bytes(g_own.at[pl.ds(0, 7)], near_recv_sem)
            near_copy.wait()
            g_copy(after, yh).start()
            g_copy(before, yh).start()
            g_copy(far, yh).start()

        return 0

    lax.fori_loop(0, 2, near_qkv, 0)
    own_g = pltpu.make_async_copy(g_own.at[:, yh], g_recv.at[yh], g_own_sem)
    own_g.start()

    def gather(source, first, stride):
        return jnp.concatenate(
            [source[pl.ds(first + r, 8, stride=stride), :] for r in range(RES)], axis=0
        ).astype(BF16)

    def chunk(src):
        return pl.ds(pl.multiple_of(src * 32, 32), 32)

    def take_qkv(src):
        wait_bytes(qkv_recv.at[src, pl.ds(0, 7)], qkv_recv_sem.at[src])
        pltpu.make_async_copy(qkv_send.at[src, g], qkv_recv.at[src, g], qkv_own_sem.at[src]).wait()
        wide[...] = qkv_recv[src].reshape(8 * 3 * HALF, 128).astype(F32)
        for s in range(SEQ_RUN // 2):
            for j, keep in enumerate((q_all, k_all, v_all)):
                keep[chunk(src), s * 128 : s * 128 + 128] = gather(wide, j * HALF + s * RES, 3 * HALF)

    def take_g(src):
        wide_g[...] = g_recv[src].reshape(8 * HALF, 128).astype(F32)
        for s in range(SEQ_RUN // 2):
            g_all[chunk(src), s * 128 : s * 128 + 128] = gather(wide_g, s * RES, HALF)

    take_qkv(yh)
    own_g.wait()
    take_g(yh)

    x_copy(far, far).wait_recv()
    do_qkv(far)

    def next_g(k, _):
        src = (yh + near_first(k)) % 4
        g_copy(src, src).wait_recv()
        take_g(src)
        return 0

    lax.fori_loop(1, 4, next_g, 0)

    def next_qkv(k, _):
        take_qkv((yh + near_first(k)) % 4)
        return 0

    lax.fori_loop(1, 4, next_qkv, 0)

    def send_part(n, product):
        part[n] = product.reshape(8, 16, 128)

        def one(k, _):
            to = (z + k) % 8
            pltpu.make_async_remote_copy(
                part.at[n, to], part_recv.at[n, z], part_send_sem.at[n], part_recv_sem.at[n],
                device_id=z_peer(to), device_id_type=MESH,
            ).start()
            return 0

        lax.fori_loop(1, 8, one, 0)
        part_recv[n, z] = part[n, z]

    def send_total(n):
        wait_bytes(part_recv.at[n, pl.ds(0, 7)], part_recv_sem.at[n])
        total[n] = jnp.sum(part_recv[n], axis=0)

        def one(k, _):
            to = (w + k) % 8
            pltpu.make_async_remote_copy(
                total.at[n], total_recv.at[n, w], total_send_sem.at[n], total_recv_sem.at[n],
                device_id=line_peer(to), device_id_type=MESH,
            ).start()
            return 0

        lax.fori_loop(1, 8, one, 0)
        total_recv[n, w] = total[n]

    def whole(n):
        wait_bytes(total_recv.at[n, pl.ds(0, 7)], total_recv_sem.at[n])
        return jnp.sum(total_recv[n], axis=0)

    send_part(0, rows_dot(q_all[...], k_all[...], NT))
    send_part(1, rows_dot(g_all[...], v_all[...], NT))
    send_total(0)
    send_total(1)
    scores = scale * whole(0)
    grown = jnp.exp(scores - jnp.max(scores, axis=-1, keepdims=True))
    probability = grown / jnp.sum(grown, axis=-1, keepdims=True)
    def send_probs(n):
        def one(k, _):
            to = (z + k) % 8
            pltpu.make_async_remote_copy(
                probs.at[n, z], probs.at[n, z], probs_send_sem.at[n], probs_recv_sem.at[n],
                device_id=z_peer(to), device_id_type=MESH,
            ).start()
            return 0

        lax.fori_loop(1, 8, one, 0)

    probs[1, z] = probability.astype(BF16)
    send_probs(1)
    prob_grad = whole(1)
    row_total = jnp.sum(probability * prob_grad, axis=-1, keepdims=True)
    probs[0, z] = (scale * probability * (prob_grad - row_total)).astype(BF16)
    send_probs(0)
    wait_bytes(probs.at[1, pl.ds(0, 7)], probs_recv_sem.at[1])
    grads[2] = rows_dot(probs[1].reshape(128, 128), g_all[...], TN)
    wait_bytes(probs.at[0, pl.ds(0, 7)], probs_recv_sem.at[0])
    score_grad = probs[0].reshape(128, 128)
    grads[0] = rows_dot(score_grad, k_all[...])
    grads[1] = rows_dot(score_grad, q_all[...], TN)

    def unit(k):
        return (yh + 2 - k // 2 + 2 * (k // 3)) % 4, (k + 3) // 4

    def pack(src, h):
        for j in range(3):
            for n in range(QUARTER):
                lanes = (h * QUARTER + n) * 128
                for r in range(RES):
                    rows = pl.ds(pl.multiple_of(src * 32 + r * 8, 8), 8)
                    wide_back[pl.ds(j * PART + n * RES + r, 8, stride=3 * PART), :] = grads[
                        j, rows, lanes : lanes + 128
                    ]
        back_send[src, h] = wide_back[...].astype(BF16).reshape(8, 3 * PART, 128)

    def send_back(src, h):
        def one(k, _):
            to = (g + k) % 8
            pltpu.make_async_remote_copy(
                back_send.at[src, h, to], back_recv.at[src, h, g],
                back_send_sem.at[src, h], back_recv_sem.at[src, h],
                device_id=head_peer(to), device_id_type=MESH,
            ).start()
            return 0

        lax.fori_loop(1, 8, one, 0)
        pltpu.make_async_copy(
            back_send.at[src, h, g], back_recv.at[src, h, g], back_own_sem.at[src, h]
        ).start()

    def early_copy(to, slot):
        return pltpu.make_async_remote_copy(
            back_send.at[to, 0], early.at[slot], early_send_sem.at[to], early_recv_sem.at[slot],
            device_id=y_peer(to), device_id_type=MESH,
        )

    def send_early(k, _):
        src = (yh + 1 + 2 * k) % 4
        pack(src, 0)
        early_copy(src, yh).start()
        return 0

    lax.fori_loop(0, 2, send_early, 0)
    pack(far, 0)
    send_back(far, 0)

    def send_second(k, _):
        src = unit(k)[0]
        pack(src, 1)
        send_back(src, 1)
        return 0

    lax.fori_loop(1, 4, send_second, 0)
    pack(yh, 0)
    send_back(yh, 0)
    pack(yh, 1)
    send_back(yh, 1)

    low_back = lax.broadcasted_iota(jnp.int32, (3 * PART, 128), 1) < HEAD_DIM

    def unfold(block):
        tops, bottoms = [], []
        for p in range(4):
            a, b = block(2 * p), block(2 * p + 1)
            tops.append(jnp.where(low_back, a, b))
            bottoms.append(pltpu.roll(jnp.where(low_back, b, a), HEAD_DIM, 1))
        top, bottom = jnp.concatenate(tops, axis=1), jnp.concatenate(bottoms, axis=1)
        return [
            jnp.concatenate([top[j * PART : (j + 1) * PART], bottom[j * PART : (j + 1) * PART]], axis=0)
            for j in range(3)
        ]

    def finish(sides, columns, keep):
        grad = None
        for side, weight in zip(sides, (wq, wk, wv)):
            term = rows_dot(side, weight[columns * (D // 2) : (columns + 1) * (D // 2), :], NT)
            grad = term if grad is None else grad + term
        pieces = grad.astype(BF16).reshape(-1, 2, QUARTER, RES, D // 2)
        for n in range(pieces.shape[0]):
            out_send[keep + n, columns] = pieces[n]

    def place(run_at, h, columns, piece):
        start = pl.multiple_of(run_at * SEQ_RUN, SEQ_RUN) + h * QUARTER + piece * (SEQ_RUN // 2)
        return out.at[pl.ds(start, QUARTER), :, pl.ds(columns * (D // 2), D // 2)]

    def arrived(src, h):
        wait_bytes(back_recv.at[src, h, pl.ds(0, 7)], back_recv_sem.at[src, h])
        pltpu.make_async_copy(
            back_send.at[src, h, g], back_recv.at[src, h, g], back_own_sem.at[src, h]
        ).wait()
        return unfold(lambda head: back_recv[src, h, head])

    def finish_unit(k, _):
        src, h = unit(k)
        sides = arrived(src, h)
        for columns in range(2):
            finish(sides, columns, k)
            for piece in range(2):
                pltpu.make_async_remote_copy(
                    out_send.at[k, columns, piece], place(yh, h, columns, piece),
                    out_send_sem.at[k], out_recv_sem.at[yh],
                    device_id=y_peer(src), device_id_type=MESH,
                ).start()

        @pl.when(k == 1)
        def _():
            def forward(n, _):
                slot = (yh + 1 + 2 * n) % 4
                early_copy(slot, slot).wait_recv()

                def one(k, _):
                    to = (g + k) % 8
                    pltpu.make_async_remote_copy(
                        early.at[slot, to], late.at[slot, g], late_send_sem.at[slot], late_recv_sem.at[slot],
                        device_id=head_peer(to), device_id_type=MESH,
                    ).start()
                    return 0

                lax.fori_loop(1, 8, one, 0)
                pltpu.make_async_copy(early.at[slot, g], late.at[slot, g], late_own_sem.at[slot]).start()
                return 0

            lax.fori_loop(0, 2, forward, 0)

        return 0

    lax.fori_loop(0, 4, finish_unit, 0)

    def both(one, two):
        return [jnp.concatenate(pair, axis=0) for pair in zip(one, two)]

    own_outs = []

    def finish_here(sides, keep, runs):
        for columns in range(2):
            finish(sides, columns, keep)
            for n, (run_at, h) in enumerate(runs):
                for piece in range(2):
                    copy = pltpu.make_async_copy(
                        out_send.at[keep + n, columns, piece], place(run_at, h, columns, piece),
                        out_own_sem.at[len(own_outs)],
                    )
                    copy.start()
                    own_outs.append(copy)

    finish_here(both(arrived(yh, 0), arrived(yh, 1)), 4, ((yh, 0), (yh, 1)))

    def arrived_late(slot):
        wait_bytes(late.at[slot, pl.ds(0, 7)], late_recv_sem.at[slot])
        pltpu.make_async_copy(early.at[slot, g], late.at[slot, g], late_own_sem.at[slot]).wait()
        return unfold(lambda head: late[slot, head])

    finish_here(both(arrived_late(after), arrived_late(before)), 6, ((after, 0), (before, 0)))

    wait_bytes(g_own.at[pl.ds(0, 7)], near_send_sem)
    for to in (after, before, far):
        x_copy(to, yh).wait_send()
    wait_bytes(g_recv.at[pl.ds(0, 3)], g_send_sem)
    wait_bytes(qkv_send.at[:, pl.ds(0, 7)], qkv_send_sem)
    for n in range(2):
        wait_bytes(part_recv.at[n, pl.ds(0, 7)], part_send_sem.at[n])
        wait_bytes(total_recv.at[n, pl.ds(0, 7)], total_send_sem.at[n])
    for n in range(2):
        wait_bytes(probs.at[n, pl.ds(0, 7)], probs_send_sem.at[n])
    def wait_back(k, _):
        src, h = unit(k)
        wait_bytes(back_send.at[src, h, pl.ds(0, 7)], back_send_sem.at[src, h])
        wait_bytes(out_send.at[k], out_send_sem.at[k])
        return 0

    lax.fori_loop(0, 4, wait_back, 0)
    for h in range(2):
        wait_bytes(back_send.at[yh, h, pl.ds(0, 7)], back_send_sem.at[yh, h])
    for slot in (after, before):
        early_copy(slot, yh).wait_send()
        wait_bytes(late.at[slot, pl.ds(0, 7)], late_send_sem.at[slot])
    wait_bytes(out.at[pl.ds(0, SEQ_RUN)], out_recv_sem.at[far])
    for slot in (after, before):
        wait_bytes(out.at[pl.ds(0, SEQ_RUN // 2)], out_recv_sem.at[slot])
    for own_out in own_outs:
        own_out.wait()


def body(activations, out_grad, w_query, w_key, w_value, w_output):
    seqs_total = activations.shape[0] * lax.axis_size("seq")
    scale = 1.0 / math.sqrt(HEAD_DIM * seqs_total)
    hbm = pl.BlockSpec(memory_space=pltpu.HBM)
    dma = pltpu.SemaphoreType.DMA
    vmem = pltpu.VMEM
    return pl.pallas_call(
        lambda *refs: kernel(scale, *refs),
        out_shape=jax.ShapeDtypeStruct(activations.shape, BF16),
        in_specs=[hbm] * 6,
        out_specs=pl.BlockSpec(memory_space=pl.ANY),
        scratch_shapes=[
            vmem((D, FEATURES), BF16),
            vmem((D, FEATURES), BF16),
            vmem((D, FEATURES), BF16),
            vmem((FEATURES, D), BF16),
            vmem((4 * SEQ_RUN, RES, D), BF16),
            vmem((4, SEQ_RUN, RES, D), BF16),
            vmem((8, 4, HALF, 128), BF16),
            vmem((8, 4, HALF, 128), BF16),
            vmem((4, 8, HALF, 128), BF16),
            vmem((4, 8, 3 * HALF, 128), BF16),
            vmem((4, 8, 3 * HALF, 128), BF16),
            vmem((8 * 3 * HALF, 128), F32),
            vmem((8 * HALF, 128), F32),
            vmem((128, SEQ_RUN * HEAD_DIM), BF16),
            vmem((128, SEQ_RUN * HEAD_DIM), BF16),
            vmem((128, SEQ_RUN * HEAD_DIM), BF16),
            vmem((128, SEQ_RUN * HEAD_DIM), BF16),
            vmem((3, 128, SEQ_RUN * HEAD_DIM), F32),
            vmem((2, 8, 16, 128), F32),
            vmem((2, 8, 16, 128), F32),
            vmem((2, 16, 128), F32),
            vmem((2, 8, 16, 128), F32),
            vmem((2, 8, 16, 128), BF16),
            vmem((8 * 3 * PART, 128), F32),
            vmem((4, 2, 8, 3 * PART, 128), BF16),
            vmem((4, 2, 8, 3 * PART, 128), BF16),
            vmem((4, 8, 3 * PART, 128), BF16),
            vmem((4, 8, 3 * PART, 128), BF16),
            vmem((8, 2, 2, QUARTER, RES, D // 2), BF16),
            dma((6,)), dma((4,)), dma((4,)), dma, dma, dma,
            dma, dma((4,)), dma, dma, dma((4,)), dma((4,)),
            dma((2,)), dma((2,)), dma((2,)), dma((2,)),
            dma((2,)), dma((2,)), dma((4, 2)), dma((4, 2)), dma((4, 2)),
            dma((4,)), dma((4,)), dma((4,)), dma((4,)), dma((4,)),
            dma((4,)), dma((4,)), dma((16,)),
        ],
        compiler_params=pltpu.CompilerParams(
            collective_id=0, has_side_effects=True, vmem_limit_bytes=54784 * 2**10
        ),
        cost_estimate=pl.CostEstimate(
            flops=2 * 10**9, bytes_accessed=5 * 10**6, transcendentals=2048
        ),
    )(activations, out_grad, w_query, w_key, w_value, w_output)


def solution(mesh):
    rows = P("seq", "res", None)
    return jax.shard_map(
        body,
        mesh=mesh,
        in_specs=(rows, rows, P(), P(), P(), P()),
        out_specs=rows,
        check_vma=False,
    )
```

```python
import math

import jax
import jax.numpy as jnp
from jax import lax
from jax.experimental import pallas as pl
from jax.experimental.pallas import tpu as pltpu
from jax.sharding import PartitionSpec as P

MESH = pl.DeviceIdType.MESH
F32, BF16 = jnp.float32, jnp.bfloat16
D = 768
FEATURES = 512
HEAD_DIM = 64
SEQ_RUN = 16
RES = 4
ROWS = SEQ_RUN * RES
HALF = ROWS // 2
QUARTER = SEQ_RUN // 4
PART = HALF // 2
NT = (((1,), (1,)), ((), ()))
TN = (((0,), (0,)), ((), ()))


def rows_dot(a, b, dims=(((1,), (0,)), ((), ()))):
    return lax.dot_general(a, b, dims, preferred_element_type=F32)


def kernel(
    scale,
    act, og, wq_hbm, wk_hbm, wv_hbm, wo_hbm,
    out,
    wq, wk, wv, wo, og_v, xr, g_near, g_own, g_recv, qkv_send, qkv_recv,
    wide, wide_g, q_all, k_all, v_all, g_all, grads,
    part, part_recv, total, total_recv, probs, wide_back, back_send, back_recv, early, late, out_send,
    load_sem, x_send_sem, x_recv_sem, near_send_sem, near_recv_sem, near_own_sem,
    g_send_sem, g_recv_sem, g_own_sem, qkv_send_sem, qkv_recv_sem, qkv_own_sem,
    part_send_sem, part_recv_sem, total_send_sem, total_recv_sem,
    probs_send_sem, probs_recv_sem, back_send_sem, back_recv_sem, back_own_sem,
    early_send_sem, early_recv_sem, late_send_sem, late_recv_sem, late_own_sem,
    out_send_sem, out_recv_sem, out_own_sem,
):
    seq, res = lax.axis_index("seq"), lax.axis_index("res")
    ylo, z = seq // 8, seq % 8
    x, yh, core = res // 8, (res // 2) % 4, res % 2
    g = x * 2 + core
    w = yh * 2 + ylo

    def y_peer(h):
        return (seq, x * 8 + h * 2 + core)

    def head_peer(h):
        return (seq, (h // 2) * 8 + yh * 2 + h % 2)

    def z_peer(k):
        return (ylo * 8 + k, res)

    def line_peer(k):
        return ((k % 2) * 8 + z, x * 8 + (k // 2) * 2 + core)

    def run(h):
        return pl.ds(pl.multiple_of(h * SEQ_RUN, SEQ_RUN), SEQ_RUN)

    def wait_bytes(ref, sem):
        pltpu.make_async_copy(ref, ref, sem).wait()

    loads = [
        pltpu.make_async_copy(og, og_v, load_sem.at[0]),
        pltpu.make_async_copy(wo_hbm, wo, load_sem.at[1]),
        pltpu.make_async_copy(act.at[run(yh)], xr.at[yh], load_sem.at[2]),
        pltpu.make_async_copy(wq_hbm, wq, load_sem.at[3]),
        pltpu.make_async_copy(wk_hbm, wk, load_sem.at[4]),
        pltpu.make_async_copy(wv_hbm, wv, load_sem.at[5]),
    ]
    for load in loads:
        load.start()

    barrier = pltpu.get_barrier_semaphore()

    def greet(k, _):
        pl.semaphore_signal(barrier, inc=1, device_id=head_peer((g + k) % 8), device_id_type=MESH)
        pl.semaphore_signal(barrier, inc=1, device_id=z_peer((z + k) % 8), device_id_type=MESH)
        pl.semaphore_signal(barrier, inc=1, device_id=line_peer((w + k) % 8), device_id_type=MESH)
        return 0

    lax.fori_loop(1, 8, greet, 0)

    pl.semaphore_wait(barrier, 21)

    def x_copy(to, slot):
        return pltpu.make_async_remote_copy(
            act.at[run(to)], xr.at[slot], x_send_sem.at[to], x_recv_sem.at[slot],
            device_id=y_peer(to), device_id_type=MESH,
        )

    after, before, far = (yh + 1) % 4, (yh + 3) % 4, (yh + 2) % 4
    x_copy(after, yh).start()
    x_copy(before, yh).start()

    low = lax.broadcasted_iota(jnp.int32, (HALF, 128), 1) < HEAD_DIM

    def fold(top, bottom):
        turned = pltpu.roll(bottom, HEAD_DIM, 1)
        return jnp.where(low, top, turned), jnp.where(low, turned, top)

    loads[0].wait()
    loads[1].wait()
    grad_rows = rows_dot(og_v[...].reshape(4 * ROWS, D), wo[...], NT).astype(BF16)
    for c in range(4):
        for p in range(4):
            pair = grad_rows[c * ROWS : (c + 1) * ROWS, p * 128 : p * 128 + 128]
            g_near[2 * p, c], g_near[2 * p + 1, c] = fold(pair[:HALF], pair[HALF:])

    def near_first(k):
        return k + k // 2 - 2 * (k // 3)

    def send_near(k, _):
        to = (g + k) % 8
        pltpu.make_async_remote_copy(
            g_near.at[to], g_own.at[g], near_send_sem, near_recv_sem,
            device_id=head_peer(to), device_id_type=MESH,
        ).start()
        return 0

    lax.fori_loop(1, 8, send_near, 0)
    near_copy = pltpu.make_async_copy(g_near.at[g], g_own.at[g], near_own_sem)
    near_copy.start()
    x_copy(far, yh).start()

    def do_qkv(src):
        rows = xr[src].reshape(ROWS, D)
        for j, weight in enumerate((wq, wk, wv)):
            a = rows_dot(rows, weight[...]).astype(BF16)
            for p in range(4):
                pair = a[:, p * 128 : p * 128 + 128]
                even, odd = fold(pair[:HALF], pair[HALF:])
                qkv_send[src, 2 * p, j * HALF : (j + 1) * HALF] = even
                qkv_send[src, 2 * p + 1, j * HALF : (j + 1) * HALF] = odd

        def one(k, _):
            to = (g + k) % 8
            pltpu.make_async_remote_copy(
                qkv_send.at[src, to], qkv_recv.at[src, g], qkv_send_sem, qkv_recv_sem.at[src],
                device_id=head_peer(to), device_id_type=MESH,
            ).start()
            return 0

        lax.fori_loop(1, 8, one, 0)
        pltpu.make_async_copy(qkv_send.at[src, g], qkv_recv.at[src, g], qkv_own_sem.at[src]).start()

    for load in loads[2:]:
        load.wait()
    do_qkv(yh)

    def g_copy(to, slot):
        return pltpu.make_async_remote_copy(
            g_own.at[:, to], g_recv.at[slot], g_send_sem, g_recv_sem.at[slot],
            device_id=y_peer(to), device_id_type=MESH,
        )

    def near_qkv(k, _):
        src = (yh + 1 + 2 * k) % 4
        x_copy(src, src).wait_recv()
        do_qkv(src)

        @pl.when(k == 0)
        def _():
            wait_bytes(g_own.at[pl.ds(0, 7)], near_recv_sem)
            near_copy.wait()
            g_copy(after, yh).start()
            g_copy(before, yh).start()
            g_copy(far, yh).start()

        return 0

    lax.fori_loop(0, 2, near_qkv, 0)
    own_g = pltpu.make_async_copy(g_own.at[:, yh], g_recv.at[yh], g_own_sem)
    own_g.start()

    def gather(source, first, stride):
        return jnp.concatenate(
            [source[pl.ds(first + r, 8, stride=stride), :] for r in range(RES)], axis=0
        ).astype(BF16)

    def chunk(src):
        return pl.ds(pl.multiple_of(src * 32, 32), 32)

    def take_qkv(src):
        wait_bytes(qkv_recv.at[src, pl.ds(0, 7)], qkv_recv_sem.at[src])
        pltpu.make_async_copy(qkv_send.at[src, g], qkv_recv.at[src, g], qkv_own_sem.at[src]).wait()
        wide[...] = qkv_recv[src].reshape(8 * 3 * HALF, 128).astype(F32)
        for s in range(SEQ_RUN // 2):
            for j, keep in enumerate((q_all, k_all, v_all)):
                keep[chunk(src), s * 128 : s * 128 + 128] = gather(wide, j * HALF + s * RES, 3 * HALF)

    def take_g(src):
        wide_g[...] = g_recv[src].reshape(8 * HALF, 128).astype(F32)
        for s in range(SEQ_RUN // 2):
            g_all[chunk(src), s * 128 : s * 128 + 128] = gather(wide_g, s * RES, HALF)

    take_qkv(yh)
    own_g.wait()
    take_g(yh)

    x_copy(far, far).wait_recv()
    do_qkv(far)

    def next_g(k, _):
        src = (yh + near_first(k)) % 4
        g_copy(src, src).wait_recv()
        take_g(src)
        return 0

    lax.fori_loop(1, 4, next_g, 0)

    def next_qkv(k, _):
        take_qkv((yh + near_first(k)) % 4)
        return 0

    lax.fori_loop(1, 4, next_qkv, 0)

    def send_part(n, product):
        part[n] = product.reshape(8, 16, 128)

        def one(k, _):
            to = (z + k) % 8
            pltpu.make_async_remote_copy(
                part.at[n, to], part_recv.at[n, z], part_send_sem.at[n], part_recv_sem.at[n],
                device_id=z_peer(to), device_id_type=MESH,
            ).start()
            return 0

        lax.fori_loop(1, 8, one, 0)
        part_recv[n, z] = part[n, z]

    def send_total(n):
        wait_bytes(part_recv.at[n, pl.ds(0, 7)], part_recv_sem.at[n])
        total[n] = jnp.sum(part_recv[n], axis=0)

        def one(k, _):
            to = (w + k) % 8
            pltpu.make_async_remote_copy(
                total.at[n], total_recv.at[n, w], total_send_sem.at[n], total_recv_sem.at[n],
                device_id=line_peer(to), device_id_type=MESH,
            ).start()
            return 0

        lax.fori_loop(1, 8, one, 0)
        total_recv[n, w] = total[n]

    def whole(n):
        wait_bytes(total_recv.at[n, pl.ds(0, 7)], total_recv_sem.at[n])
        return jnp.sum(total_recv[n], axis=0)

    send_part(0, rows_dot(q_all[...], k_all[...], NT))
    send_part(1, rows_dot(g_all[...], v_all[...], NT))
    send_total(0)
    send_total(1)
    scores = scale * whole(0)
    grown = jnp.exp(scores - jnp.max(scores, axis=-1, keepdims=True))
    probability = grown / jnp.sum(grown, axis=-1, keepdims=True)
    def send_probs(n):
        def one(k, _):
            to = (z + k) % 8
            pltpu.make_async_remote_copy(
                probs.at[n, z], probs.at[n, z], probs_send_sem.at[n], probs_recv_sem.at[n],
                device_id=z_peer(to), device_id_type=MESH,
            ).start()
            return 0

        lax.fori_loop(1, 8, one, 0)

    probs[1, z] = probability.astype(BF16)
    send_probs(1)
    prob_grad = whole(1)
    row_total = jnp.sum(probability * prob_grad, axis=-1, keepdims=True)
    probs[0, z] = (scale * probability * (prob_grad - row_total)).astype(BF16)
    send_probs(0)
    wait_bytes(probs.at[1, pl.ds(0, 7)], probs_recv_sem.at[1])
    grads[2] = rows_dot(probs[1].reshape(128, 128), g_all[...], TN)
    wait_bytes(probs.at[0, pl.ds(0, 7)], probs_recv_sem.at[0])
    score_grad = probs[0].reshape(128, 128)
    grads[0] = rows_dot(score_grad, k_all[...])
    grads[1] = rows_dot(score_grad, q_all[...], TN)

    def unit(k):
        return (yh + 2 - k // 2 + 2 * (k // 3)) % 4, (k + 3) // 4

    def pack(src, h):
        for j in range(3):
            for n in range(QUARTER):
                lanes = (h * QUARTER + n) * 128
                for r in range(RES):
                    rows = pl.ds(pl.multiple_of(src * 32 + r * 8, 8), 8)
                    wide_back[pl.ds(j * PART + n * RES + r, 8, stride=3 * PART), :] = grads[
                        j, rows, lanes : lanes + 128
                    ]
        back_send[src, h] = wide_back[...].astype(BF16).reshape(8, 3 * PART, 128)

    def send_back(src, h):
        def one(k, _):
            to = (g + k) % 8
            pltpu.make_async_remote_copy(
                back_send.at[src, h, to], back_recv.at[src, h, g],
                back_send_sem.at[src, h], back_recv_sem.at[src, h],
                device_id=head_peer(to), device_id_type=MESH,
            ).start()
            return 0

        lax.fori_loop(1, 8, one, 0)
        pltpu.make_async_copy(
            back_send.at[src, h, g], back_recv.at[src, h, g], back_own_sem.at[src, h]
        ).start()

    def early_copy(to, slot):
        return pltpu.make_async_remote_copy(
            back_send.at[to, 0], early.at[slot], early_send_sem.at[to], early_recv_sem.at[slot],
            device_id=y_peer(to), device_id_type=MESH,
        )

    def send_early(k, _):
        src = (yh + 1 + 2 * k) % 4
        pack(src, 0)
        early_copy(src, yh).start()
        return 0

    lax.fori_loop(0, 2, send_early, 0)
    pack(far, 0)
    send_back(far, 0)

    def send_second(k, _):
        src = unit(k)[0]
        pack(src, 1)
        send_back(src, 1)
        return 0

    lax.fori_loop(1, 4, send_second, 0)
    pack(yh, 0)
    send_back(yh, 0)
    pack(yh, 1)
    send_back(yh, 1)

    low_back = lax.broadcasted_iota(jnp.int32, (3 * PART, 128), 1) < HEAD_DIM

    def unfold(block):
        tops, bottoms = [], []
        for p in range(4):
            a, b = block(2 * p), block(2 * p + 1)
            tops.append(jnp.where(low_back, a, b))
            bottoms.append(pltpu.roll(jnp.where(low_back, b, a), HEAD_DIM, 1))
        top, bottom = jnp.concatenate(tops, axis=1), jnp.concatenate(bottoms, axis=1)
        return [
            jnp.concatenate([top[j * PART : (j + 1) * PART], bottom[j * PART : (j + 1) * PART]], axis=0)
            for j in range(3)
        ]

    def finish(sides, columns, keep):
        grad = None
        for side, weight in zip(sides, (wq, wk, wv)):
            term = rows_dot(side, weight[...], NT)
            grad = term if grad is None else grad + term
        pieces = grad.astype(BF16).reshape(-1, 2, QUARTER, RES, D)
        for n in range(pieces.shape[0]):
            out_send[keep + n, columns] = pieces[n]

    def place(run_at, h, columns, piece):
        start = pl.multiple_of(run_at * SEQ_RUN, SEQ_RUN) + h * QUARTER + piece * (SEQ_RUN // 2)
        return out.at[pl.ds(start, QUARTER)]

    def arrived(src, h):
        wait_bytes(back_recv.at[src, h, pl.ds(0, 7)], back_recv_sem.at[src, h])
        pltpu.make_async_copy(
            back_send.at[src, h, g], back_recv.at[src, h, g], back_own_sem.at[src, h]
        ).wait()
        return unfold(lambda head: back_recv[src, h, head])

    def finish_unit(k, _):
        src, h = unit(k)
        sides = arrived(src, h)
        for columns in range(1):
            finish(sides, columns, k)
            for piece in range(2):
                pltpu.make_async_remote_copy(
                    out_send.at[k, columns, piece], place(yh, h, columns, piece),
                    out_send_sem.at[k], out_recv_sem.at[yh],
                    device_id=y_peer(src), device_id_type=MESH,
                ).start()

        @pl.when(k == 1)
        def _():
            def forward(n, _):
                slot = (yh + 1 + 2 * n) % 4
                early_copy(slot, slot).wait_recv()

                def one(k, _):
                    to = (g + k) % 8
                    pltpu.make_async_remote_copy(
                        early.at[slot, to], late.at[slot, g], late_send_sem.at[slot], late_recv_sem.at[slot],
                        device_id=head_peer(to), device_id_type=MESH,
                    ).start()
                    return 0

                lax.fori_loop(1, 8, one, 0)
                pltpu.make_async_copy(early.at[slot, g], late.at[slot, g], late_own_sem.at[slot]).start()
                return 0

            lax.fori_loop(0, 2, forward, 0)

        return 0

    lax.fori_loop(0, 4, finish_unit, 0)

    def both(one, two):
        return [jnp.concatenate(pair, axis=0) for pair in zip(one, two)]

    own_outs = []

    def finish_here(sides, keep, runs):
        for columns in range(1):
            finish(sides, columns, keep)
            for n, (run_at, h) in enumerate(runs):
                for piece in range(2):
                    copy = pltpu.make_async_copy(
                        out_send.at[keep + n, columns, piece], place(run_at, h, columns, piece),
                        out_own_sem.at[len(own_outs)],
                    )
                    copy.start()
                    own_outs.append(copy)

    finish_here(both(arrived(yh, 0), arrived(yh, 1)), 4, ((yh, 0), (yh, 1)))

    def arrived_late(slot):
        wait_bytes(late.at[slot, pl.ds(0, 7)], late_recv_sem.at[slot])
        pltpu.make_async_copy(early.at[slot, g], late.at[slot, g], late_own_sem.at[slot]).wait()
        return unfold(lambda head: late[slot, head])

    finish_here(both(arrived_late(after), arrived_late(before)), 6, ((after, 0), (before, 0)))

    wait_bytes(g_own.at[pl.ds(0, 7)], near_send_sem)
    for to in (after, before, far):
        x_copy(to, yh).wait_send()
    wait_bytes(g_recv.at[pl.ds(0, 3)], g_send_sem)
    wait_bytes(qkv_send.at[:, pl.ds(0, 7)], qkv_send_sem)
    for n in range(2):
        wait_bytes(part_recv.at[n, pl.ds(0, 7)], part_send_sem.at[n])
        wait_bytes(total_recv.at[n, pl.ds(0, 7)], total_send_sem.at[n])
    for n in range(2):
        wait_bytes(probs.at[n, pl.ds(0, 7)], probs_send_sem.at[n])
    def wait_back(k, _):
        src, h = unit(k)
        wait_bytes(back_send.at[src, h, pl.ds(0, 7)], back_send_sem.at[src, h])
        wait_bytes(out_send.at[k], out_send_sem.at[k])
        return 0

    lax.fori_loop(0, 4, wait_back, 0)
    for h in range(2):
        wait_bytes(back_send.at[yh, h, pl.ds(0, 7)], back_send_sem.at[yh, h])
    for slot in (after, before):
        early_copy(slot, yh).wait_send()
        wait_bytes(late.at[slot, pl.ds(0, 7)], late_send_sem.at[slot])
    wait_bytes(out.at[pl.ds(0, SEQ_RUN)], out_recv_sem.at[far])
    for slot in (after, before):
        wait_bytes(out.at[pl.ds(0, SEQ_RUN // 2)], out_recv_sem.at[slot])
    for own_out in own_outs:
        own_out.wait()


def body(activations, out_grad, w_query, w_key, w_value, w_output):
    seqs_total = activations.shape[0] * lax.axis_size("seq")
    scale = 1.0 / math.sqrt(HEAD_DIM * seqs_total)
    hbm = pl.BlockSpec(memory_space=pltpu.HBM)
    dma = pltpu.SemaphoreType.DMA
    vmem = pltpu.VMEM
    return pl.pallas_call(
        lambda *refs: kernel(scale, *refs),
        out_shape=jax.ShapeDtypeStruct(activations.shape, BF16),
        in_specs=[hbm] * 6,
        out_specs=pl.BlockSpec(memory_space=pl.ANY),
        scratch_shapes=[
            vmem((D, FEATURES), BF16),
            vmem((D, FEATURES), BF16),
            vmem((D, FEATURES), BF16),
            vmem((FEATURES, D), BF16),
            vmem((4 * SEQ_RUN, RES, D), BF16),
            vmem((4, SEQ_RUN, RES, D), BF16),
            vmem((8, 4, HALF, 128), BF16),
            vmem((8, 4, HALF, 128), BF16),
            vmem((4, 8, HALF, 128), BF16),
            vmem((4, 8, 3 * HALF, 128), BF16),
            vmem((4, 8, 3 * HALF, 128), BF16),
            vmem((8 * 3 * HALF, 128), F32),
            vmem((8 * HALF, 128), F32),
            vmem((128, SEQ_RUN * HEAD_DIM), BF16),
            vmem((128, SEQ_RUN * HEAD_DIM), BF16),
            vmem((128, SEQ_RUN * HEAD_DIM), BF16),
            vmem((128, SEQ_RUN * HEAD_DIM), BF16),
            vmem((3, 128, SEQ_RUN * HEAD_DIM), F32),
            vmem((2, 8, 16, 128), F32),
            vmem((2, 8, 16, 128), F32),
            vmem((2, 16, 128), F32),
            vmem((2, 8, 16, 128), F32),
            vmem((2, 8, 16, 128), BF16),
            vmem((8 * 3 * PART, 128), F32),
            vmem((4, 2, 8, 3 * PART, 128), BF16),
            vmem((4, 2, 8, 3 * PART, 128), BF16),
            vmem((4, 8, 3 * PART, 128), BF16),
            vmem((4, 8, 3 * PART, 128), BF16),
            vmem((8, 1, 2, QUARTER, RES, D), BF16),
            dma((6,)), dma((4,)), dma((4,)), dma, dma, dma,
            dma, dma((4,)), dma, dma, dma((4,)), dma((4,)),
            dma((2,)), dma((2,)), dma((2,)), dma((2,)),
            dma((2,)), dma((2,)), dma((4, 2)), dma((4, 2)), dma((4, 2)),
            dma((4,)), dma((4,)), dma((4,)), dma((4,)), dma((4,)),
            dma((4,)), dma((4,)), dma((16,)),
        ],
        compiler_params=pltpu.CompilerParams(
            collective_id=0, has_side_effects=True, vmem_limit_bytes=54784 * 2**10
        ),
        cost_estimate=pl.CostEstimate(
            flops=2 * 10**9, bytes_accessed=5 * 10**6, transcendentals=2048
        ),
    )(activations, out_grad, w_query, w_key, w_value, w_output)


def solution(mesh):
    rows = P("seq", "res", None)
    return jax.shard_map(
        body,
        mesh=mesh,
        in_specs=(rows, rows, P(), P(), P(), P()),
        out_specs=rows,
        check_vma=False,
    )
```
